128 devices in a mesh: seq: 32 (over x, z, y_lo), tp: 4 (over y_hi, core).
Axes of the slice: x: 4, y: 4 (y_hi: 2, y_lo: 2; y = y_hi * 2 + y_lo), z: 4, core: 2. Of those that a mesh axis runs over, the one named last changes fastest.
Arguments:
- context: bfloat16 [65536, 2048], P('seq'), may hold values from -40 to 40
- latent_in: bfloat16 [1024, 2048], P('seq'), may hold values from -24 to 24
- cutoff: int32 [1024], replicated, may hold values from 0 to 65535, as said below
- wq_cross: bfloat16 [2048, 2048], P(None, 'tp'), may hold values from -0.6 to 0.6
- wk_cross: bfloat16 [2048, 2048], P(None, 'tp'), may hold values from -0.6 to 0.6
- wv_cross: bfloat16 [2048, 2048], P(None, 'tp'), may hold values from -0.125 to 0.125
- wo_cross: bfloat16 [2048, 2048], P('tp'), may hold values from -0.125 to 0.125
- wq_self: bfloat16 [2048, 2048], P(None, 'tp'), may hold values from -0.6 to 0.6
- wk_self: bfloat16 [2048, 2048], P(None, 'tp'), may hold values from -0.6 to 0.6
- wv_self: bfloat16 [2048, 2048], P(None, 'tp'), may hold values from -0.125 to 0.125
- wo_self: bfloat16 [2048, 2048], P('tp'), may hold values from -0.125 to 0.125
Outputs:
- latent_out: bfloat16 [1024, 2048], P('seq')
The draws below stay inside these ranges and needn't reach their ends.
Inputs may be any that keep to these rules, and one draw needn't show every extreme that they name: `cutoff`: strictly increasing; the last entry is 65535.
All inputs are finite; a program needn't handle non-finite values.
Results may differ from the reference program's by a relative error of at most 0.012.
Values may be sent and summed in bfloat16 or wider, within the bound.
No kernel may reach another device: no remote copies, remote signals or barrier semaphores. Data moves between devices by JAX's collectives and lax.ppermute only.
A program may use at most 192 MiB of HBM per device.

```python
import jax
import jax.numpy as jnp
from jax import lax

D = 2048
HEADS = 16
HEAD_DIM = 128
LATENTS = 1024
CONTEXT = 65536


def shared_context(key):
    return jax.random.normal(jax.random.fold_in(key, 101), (CONTEXT, D), jnp.float32)


def drawn_weight(own):
    return jnp.clip(own * D ** (-0.5), -0.59375, 0.59375)


def draw_context(key, part):
    base = shared_context(key)
    return jnp.clip(base, -4.0, 4.0).astype(jnp.bfloat16)


def draw_latent_in(key, part):
    key = jax.random.fold_in(key, 2)
    key_noise = jax.random.fold_in(key, 0)
    noise = jax.random.normal(key_noise, (LATENTS, D), jnp.float32)
    return jnp.clip(noise, -4.0, 4.0).astype(jnp.bfloat16)


def draw_cutoff(key, part):
    key = jax.random.fold_in(key, 7)
    picks = jax.random.permutation(key, CONTEXT - 1)[:LATENTS - 1]
    ordered = jnp.sort(picks).astype(jnp.int32)
    return jnp.concatenate([ordered, jnp.full((1,), CONTEXT - 1, jnp.int32)])


def draw_wq_cross(key, part):
    key = jax.random.fold_in(key, 3)
    own = jax.random.normal(key, (D, D), jnp.float32)
    return drawn_weight(own).astype(jnp.bfloat16)


def draw_wk_cross(key, part):
    key = jax.random.fold_in(key, 4)
    own = jax.random.normal(key, (D, D), jnp.float32)
    return drawn_weight(own).astype(jnp.bfloat16)


def draw_wq_self(key, part):
    key = jax.random.fold_in(key, 5)
    own = jax.random.normal(key, (D, D), jnp.float32)
    return drawn_weight(own).astype(jnp.bfloat16)


def draw_wk_self(key, part):
    key = jax.random.fold_in(key, 6)
    own = jax.random.normal(key, (D, D), jnp.float32)
    return drawn_weight(own).astype(jnp.bfloat16)


def levels(key, shape, pieces, least, top_value):
    def one(position, blocks):
        steps = jax.random.uniform(jax.random.fold_in(jax.random.fold_in(key, 6), position), (blocks,), jnp.float32, least / len(pieces), top_value / len(pieces))
        return jnp.repeat(jnp.exp(steps), shape[position] // blocks).reshape((-1,) + (1,) * (len(shape) - position - 1))

    level = one(*pieces[0])
    for cut in pieces[1:]:
        level = level * one(*cut)
    return level


def normal_values(key, dims, scale, most, pieces=(), held_as=jnp.bfloat16):
    drawn = jax.random.normal(key, dims, jnp.float32) * scale
    if len(pieces) > 0:
        drawn = levels(key, dims, pieces, -0.22, 0.18) * drawn
    return jnp.clip(drawn, min=-most, max=most).astype(held_as)


def setup_inputs(seed: int = 0) -> dict:
    key_of = jax.random.split(jax.random.key(seed), 12)
    context = draw_context(jax.random.fold_in(key_of[11], 71), 0)
    latent_in = draw_latent_in(jax.random.fold_in(key_of[11], 71), 0)
    cutoff = draw_cutoff(jax.random.fold_in(key_of[11], 71), 0)
    wq_cross = draw_wq_cross(jax.random.fold_in(key_of[11], 71), 0)
    wk_cross = draw_wk_cross(jax.random.fold_in(key_of[11], 71), 0)
    wv_cross = normal_values(key_of[5], (D, D), D ** -0.5, 0.125, ((1, 4),))
    wo_cross = normal_values(key_of[6], (D, D), D ** -0.5, 0.125, ((0, 4),))
    wq_self = draw_wq_self(jax.random.fold_in(key_of[11], 71), 0)
    wk_self = draw_wk_self(jax.random.fold_in(key_of[11], 71), 0)
    wv_self = normal_values(key_of[9], (D, D), D ** -0.5, 0.125, ((1, 4),))
    wo_self = normal_values(key_of[10], (D, D), D ** -0.5, 0.125, ((0, 4),))
    return {"context": context, "latent_in": latent_in, "cutoff": cutoff, "wq_cross": wq_cross, "wk_cross": wk_cross, "wv_cross": wv_cross, "wo_cross": wo_cross, "wq_self": wq_self, "wk_self": wk_self, "wv_self": wv_self, "wo_self": wo_self}


EPSILON = 1e-05
MASKED_SCORE = -1e+30

def normalize(tensor):
    tensor = tensor.astype(jnp.float32)
    return tensor * lax.rsqrt(lax.optimization_barrier(jnp.mean(tensor * tensor, axis=-1, keepdims=True)) + EPSILON)

def attend(query, keys_one, values_one, visible):
    scores = jnp.dot(query, keys_one.T, preferred_element_type=jnp.float32) * HEAD_DIM ** (-0.5)
    scores = jnp.where(visible, scores, MASKED_SCORE)
    row_peak = lax.optimization_barrier(jnp.max(scores, axis=1, keepdims=True))
    probs = jnp.where(visible, jnp.exp(scores - row_peak), 0.0)
    row_total = lax.optimization_barrier(jnp.sum(probs, axis=1, keepdims=True))
    weighted = jnp.dot(probs.astype(jnp.bfloat16), values_one, preferred_element_type=jnp.float32)
    return (weighted / row_total).astype(jnp.bfloat16)

def by_heads(query, keys_all, values_all, visible):
    row_count = query.shape[0]
    heads_q = query.reshape(row_count, HEADS, HEAD_DIM).transpose(1, 0, 2)
    heads_k = keys_all.reshape(keys_all.shape[0], HEADS, HEAD_DIM).transpose(1, 0, 2)
    heads_v = values_all.reshape(values_all.shape[0], HEADS, HEAD_DIM).transpose(1, 0, 2)

    def one_head(triple):
        return attend(triple[0], triple[1], triple[2], visible)
    result = lax.map(one_head, (heads_q, heads_k, heads_v))
    return result.transpose(1, 0, 2).reshape(row_count, HEADS * HEAD_DIM)

def reference(context, latent_in, cutoff, wq_cross, wk_cross, wv_cross, wo_cross, wq_self, wk_self, wv_self, wo_self):
    ctx_norm = normalize(context).astype(jnp.bfloat16)
    ctx_keys = jnp.dot(ctx_norm, wk_cross, preferred_element_type=jnp.float32).astype(jnp.bfloat16)
    ctx_values = jnp.dot(ctx_norm, wv_cross, preferred_element_type=jnp.float32).astype(jnp.bfloat16)
    lat_norm = normalize(latent_in).astype(jnp.bfloat16)
    queries = jnp.dot(lat_norm, wq_cross, preferred_element_type=jnp.float32).astype(jnp.bfloat16)
    positions = jnp.arange(ctx_keys.shape[0], dtype=jnp.int32)
    visible = positions[None, :] <= cutoff[:, None]
    cross_out = by_heads(queries, ctx_keys, ctx_values, visible)
    latent_state = latent_in.astype(jnp.float32) + jnp.dot(cross_out, wo_cross, preferred_element_type=jnp.float32)
    state_norm = normalize(latent_state).astype(jnp.bfloat16)
    self_queries = jnp.dot(state_norm, wq_self, preferred_element_type=jnp.float32).astype(jnp.bfloat16)
    self_keys = jnp.dot(state_norm, wk_self, preferred_element_type=jnp.float32).astype(jnp.bfloat16)
    self_values = jnp.dot(state_norm, wv_self, preferred_element_type=jnp.float32).astype(jnp.bfloat16)
    key_order = jnp.arange(LATENTS, dtype=jnp.int32)
    causal = key_order[None, :] <= key_order[:, None]
    self_out = by_heads(self_queries, self_keys, self_values, causal)
    return (latent_state + jnp.dot(self_out, wo_self, preferred_element_type=jnp.float32)).astype(jnp.bfloat16)
```

```python
import functools

import jax
import jax.numpy as jnp
from jax import lax
from jax.experimental import pallas as pl
from jax.experimental.pallas import tpu as pltpu
from jax.sharding import Mesh, PartitionSpec as P

HEAD_DIM = 128
EPSILON = 1e-05
MASKED_SCORE = -1e30
LOG2E = 1.4426950408889634
MIB = 1 << 20
F32 = jnp.float32
BF16 = jnp.bfloat16

VMEM = pl.BlockSpec(memory_space=pltpu.VMEM)
SMEM = pl.BlockSpec(memory_space=pltpu.SMEM)


def shape_of(dims, dtype=BF16):
    return jax.ShapeDtypeStruct(dims, dtype)


def params(mib):
    return pltpu.CompilerParams(vmem_limit_bytes=mib * MIB)


def cost(flops, nbytes, trans=0):
    return pl.CostEstimate(flops=flops, bytes_accessed=nbytes, transcendentals=trans)


def dot(a, b):
    return jnp.dot(a, b, preferred_element_type=F32)


def dot_t(a, b):
    return lax.dot_general(a, b, (((1,), (1,)), ((), ())), preferred_element_type=F32)


def inv_rms(tile):
    return lax.rsqrt(jnp.mean(tile * tile, axis=-1, keepdims=True) + EPSILON)


def query_kernel(latent_ref, wq_ref, out_ref):
    tile = latent_ref[...].astype(F32)
    normed = (tile * inv_rms(tile)).astype(BF16)
    factor = HEAD_DIM ** (-0.5) * LOG2E
    out_ref[...] = (dot(normed, wq_ref[...]) * factor).astype(BF16)


def project_queries(latent_in, wq):
    rows, width = latent_in.shape
    cols = wq.shape[1]
    return pl.pallas_call(
        query_kernel,
        out_shape=shape_of((rows, cols)),
        in_specs=[VMEM, VMEM],
        out_specs=VMEM,
        compiler_params=params(16),
        cost_estimate=cost(2 * rows * width * cols, 2 * width * cols),
        name="queries",
    )(latent_in, wq)


def context_kernel(context_ref, w_ref, out_ref):
    tile = context_ref[...]
    wide = tile.astype(F32)
    out_ref[...] = (dot(tile, w_ref[...]) * inv_rms(wide)).astype(BF16)


def project_context(context, weight, name):
    rows, width = context.shape
    cols = weight.shape[1]
    step = min(256, rows)
    return pl.pallas_call(
        context_kernel,
        out_shape=shape_of((rows, cols)),
        grid=(rows // step,),
        in_specs=[
            pl.BlockSpec((step, width), lambda i: (i, 0)),
            pl.BlockSpec((width, cols), lambda i: (0, 0)),
        ],
        out_specs=pl.BlockSpec((step, cols), lambda i: (i, 0)),
        compiler_params=params(24),
        cost_estimate=cost(2 * rows * width * cols, 2 * (rows * width + width * cols)),
        name=name,
    )(context, weight)


def put_total(stat, lane, head, total):
    high = total.astype(BF16).astype(F32)
    rest = total - high
    mid = rest.astype(BF16).astype(F32)
    low = rest - mid
    stat = jnp.where(lane == 3 * head, high, stat)
    stat = jnp.where(lane == 3 * head + 1, mid, stat)
    return jnp.where(lane == 3 * head + 2, low, stat)


def spread_matrix(heads):
    row = lax.broadcasted_iota(jnp.int32, (HEAD_DIM, heads * HEAD_DIM), 0)
    head = lax.shift_right_logical(
        lax.broadcasted_iota(jnp.int32, (HEAD_DIM, heads * HEAD_DIM), 1), 7
    )
    inside = (row >= 3 * head) & (row < 3 * head + 3)
    return jnp.where(inside, 1.0, 0.0).astype(BF16)


def cross_kernel(offset, ids_ref, cutoff_ref, q_ref, k_ref, v_ref, cut_ref, out_ref):
    rows, cols = q_ref.shape
    heads = cols // HEAD_DIM
    places = k_ref.shape[0]
    block = lax.rem(ids_ref[0] + offset, 4)
    start = block * rows
    first_pos = ids_ref[2]
    lowest = cutoff_ref[start] - first_pos
    highest = cutoff_ref[start + rows - 1] - first_pos
    lane = lax.broadcasted_iota(jnp.int32, (rows, HEAD_DIM), 1)

    @pl.when(highest < 0)
    def _():
        out_ref[:, :cols] = jnp.zeros((rows, cols), BF16)
        stat = jnp.zeros((rows, HEAD_DIM), F32)
        for head in range(heads):
            stat = put_total(stat, lane, head, jnp.full((rows, HEAD_DIM), MASKED_SCORE, F32))
        out_ref[:, cols:] = stat.astype(BF16)

    def attend(masked):
        stat = jnp.zeros((rows, HEAD_DIM), F32)
        ones = jnp.ones((places, HEAD_DIM), BF16)
        if masked:
            cut = cut_ref[pl.ds(pl.multiple_of(start, 128), rows), :] - first_pos
        for head in range(heads):
            span = slice(head * HEAD_DIM, (head + 1) * HEAD_DIM)
            scores = dot_t(q_ref[:, span], k_ref[:, span])
            if masked:
                order = lax.broadcasted_iota(jnp.int32, (rows, places), 1)
                seen = order <= jnp.concatenate([cut] * (places // HEAD_DIM), axis=1)
                scores = jnp.where(seen, scores, MASKED_SCORE)
            peak = jnp.max(scores, axis=1, keepdims=True)
            probs = jnp.exp2(scores - peak).astype(BF16)
            both = dot(probs, jnp.concatenate([v_ref[:, span], ones], axis=1))
            total = both[:, HEAD_DIM:]
            out_ref[:, span] = (both[:, :HEAD_DIM] / total).astype(BF16)
            whole = jnp.log2(total) + peak
            if masked:
                whole = jnp.where(cut >= 0, whole, MASKED_SCORE)
            stat = put_total(stat, lane, head, whole)
        out_ref[:, cols:] = stat.astype(BF16)

    @pl.when((highest >= 0) & (lowest < places - 1))
    def _():
        attend(True)

    @pl.when(lowest >= places - 1)
    def _():
        attend(False)


def cross_attend(offset, ids, cutoff, queries, keys, values, cut_wide):
    rows, cols = queries.shape
    places = keys.shape[0]
    return pl.pallas_call(
        functools.partial(cross_kernel, offset),
        out_shape=shape_of((rows, cols + HEAD_DIM)),
        in_specs=[SMEM, SMEM, VMEM, VMEM, VMEM, VMEM],
        out_specs=VMEM,
        compiler_params=params(40),
        cost_estimate=cost(8 * rows * places * cols, 4 * places * cols, rows * places * 4),
        name="cross",
    )(ids, cutoff, queries, keys, values, cut_wide)


def blend(parts, spread, heads):
    cols = heads * HEAD_DIM
    totals = [dot(part[:, cols:], spread) for part in parts]
    peak = functools.reduce(jnp.maximum, totals)
    weights = [jnp.exp2(total - peak) for total in totals]
    weight_sum = functools.reduce(jnp.add, weights)
    mixed = functools.reduce(
        jnp.add, [w * part[:, :cols].astype(F32) for w, part in zip(weights, parts)]
    )
    return mixed / weight_sum, peak + jnp.log2(weight_sum)


def blend_kernel(a_ref, b_ref, c_ref, d_ref, out_ref):
    rows, width = a_ref.shape
    heads = width // HEAD_DIM - 1
    cols = heads * HEAD_DIM
    mixed, whole = blend(
        [a_ref[...], b_ref[...], c_ref[...], d_ref[...]], spread_matrix(heads), heads
    )
    out_ref[:, :cols] = mixed.astype(BF16)
    lane = lax.broadcasted_iota(jnp.int32, (rows, HEAD_DIM), 1)
    stat = jnp.zeros((rows, HEAD_DIM), F32)
    for head in range(heads):
        stat = put_total(stat, lane, head, whole[:, head * HEAD_DIM : (head + 1) * HEAD_DIM])
    out_ref[:, cols:] = stat.astype(BF16)


def blend_parts(parts):
    return pl.pallas_call(
        blend_kernel,
        out_shape=shape_of(parts[0].shape),
        in_specs=[VMEM] * 4,
        out_specs=VMEM,
        compiler_params=params(16),
        name="blend",
    )(*parts)


def cross_output_kernel(parts_ref, wo_ref, out_ref):
    heads = parts_ref.shape[2] // HEAD_DIM - 1
    parts = [parts_ref[i] for i in range(parts_ref.shape[0])]
    mixed, _ = blend(parts, spread_matrix(heads), heads)
    out_ref[...] = dot(mixed.astype(BF16), wo_ref[...]).astype(BF16)


def cross_output(parts, wo):
    return pl.pallas_call(
        cross_output_kernel,
        out_shape=shape_of((parts.shape[1], wo.shape[1])),
        in_specs=[VMEM] * 2,
        out_specs=VMEM,
        compiler_params=params(16),
        name="cross_output",
    )(parts, wo)


def self_project_kernel(
    ids_ref, latent_ref, one_ref, two_ref, wq_ref, wk_ref, wv_ref, state_ref, *rest
):
    outs, held = rest[:4], rest[4]
    rows, cols = held.shape[1:]
    state = latent_ref[...].astype(F32) + (one_ref[...].astype(F32) + two_ref[...].astype(F32))
    state_ref[...] = state
    normed = (state * inv_rms(state)).astype(BF16)
    held[0] = (dot(normed, wq_ref[...]) * (HEAD_DIM ** (-0.5) * LOG2E)).astype(BF16)
    held[1] = dot(normed, wk_ref[...]).astype(BF16)
    held[2] = dot(normed, wv_ref[...]).astype(BF16)
    for offset in range(4):
        head = lax.rem(ids_ref[0] + offset, 4)
        span = pl.ds(pl.multiple_of(head * HEAD_DIM, HEAD_DIM), HEAD_DIM)
        for part in range(3):
            outs[offset][:, part * HEAD_DIM : (part + 1) * HEAD_DIM] = held[part, :, span]


def self_project(ids, latent_in, one, two, wq, wk, wv):
    rows, width = latent_in.shape
    return pl.pallas_call(
        self_project_kernel,
        out_shape=[shape_of((rows, width), F32)] + [shape_of((rows, 3 * HEAD_DIM))] * 4,
        in_specs=[SMEM] + [VMEM] * 6,
        out_specs=[VMEM] * 5,
        scratch_shapes=[pltpu.VMEM((3, rows, wq.shape[1]), BF16)],
        compiler_params=params(24),
        name="self_project",
    )(ids, latent_in, one, two, wq, wk, wv)


def self_kernel(ids_ref, a_ref, b_ref, c_ref, d_ref, kv_ref, *outs):
    rows = a_ref.shape[0]
    groups, group_rows, _ = kv_ref.shape
    own_x, own_zy = ids_ref[0], ids_ref[1]
    q = jnp.concatenate([ref[:, :HEAD_DIM] for ref in (a_ref, b_ref, c_ref, d_ref)], axis=0)
    k = jnp.concatenate([kv_ref[i, :, :HEAD_DIM] for i in range(groups)], axis=0)
    v = jnp.concatenate([kv_ref[i, :, HEAD_DIM:] for i in range(groups)], axis=0)
    scores = dot_t(q, k)
    q_row = lax.broadcasted_iota(jnp.int32, scores.shape, 0)
    k_row = lax.broadcasted_iota(jnp.int32, scores.shape, 1)
    shift = rows.bit_length() - 1
    q_x = (own_x - (q_row >> shift)) & 3
    q_place = (q_x * groups + own_zy) * rows + (q_row & (rows - 1))
    group = k_row >> (group_rows.bit_length() - 1)
    k_x = (own_x - (k_row >> shift)) & 3
    k_place = (k_x * groups + group) * rows + (k_row & (rows - 1))
    scores = jnp.where(k_place <= q_place, scores, MASKED_SCORE)
    peak = jnp.max(scores, axis=1, keepdims=True)
    probs = jnp.exp2(scores - peak).astype(BF16)
    both = dot(probs, jnp.concatenate([v, jnp.ones(v.shape, BF16)], axis=1))
    result = (both[:, :HEAD_DIM] / both[:, HEAD_DIM:]).astype(BF16)
    for offset in range(4):
        outs[offset][...] = result[offset * rows : (offset + 1) * rows]


def self_attend(ids, parts, kv):
    rows = parts[0].shape[0]
    return pl.pallas_call(
        self_kernel,
        out_shape=[shape_of((rows, HEAD_DIM))] * 4,
        in_specs=[SMEM] + [VMEM] * 5,
        out_specs=[VMEM] * 4,
        compiler_params=params(16),
        name="self_attend",
    )(ids, *parts, kv)


def self_output_kernel(ids_ref, a_ref, b_ref, c_ref, d_ref, wo_ref, out_ref, held):
    for offset, ref in enumerate((a_ref, b_ref, c_ref, d_ref)):
        head = lax.rem(ids_ref[0] + offset, 4)
        held[:, pl.ds(pl.multiple_of(head * HEAD_DIM, HEAD_DIM), HEAD_DIM)] = ref[...]
    out_ref[...] = dot(held[...], wo_ref[...]).astype(BF16)


def self_output(ids, parts, wo):
    rows = parts[0].shape[0]
    return pl.pallas_call(
        self_output_kernel,
        out_shape=shape_of((rows, wo.shape[1])),
        in_specs=[SMEM] + [VMEM] * 5,
        out_specs=VMEM,
        scratch_shapes=[pltpu.VMEM((rows, wo.shape[0]), BF16)],
        compiler_params=params(16),
        name="self_output",
    )(ids, *parts, wo)


def moved(tensor, axis, size, offset):
    return lax.ppermute(tensor, axis, [(i, (i + offset) % size) for i in range(size)])


def summed_over_tp(part):
    other = moved(part, "core", 2, 1)
    pair = (part.astype(F32) + other.astype(F32)).astype(BF16)
    return pair, moved(pair, "y_hi", 2, 1)


def on_device(
    context,
    latent_in,
    cutoff,
    wq_cross,
    wk_cross,
    wv_cross,
    wo_cross,
    wq_self,
    wk_self,
    wv_self,
    wo_self,
):
    x = lax.axis_index("x")
    zy = lax.axis_index("z") * 2 + lax.axis_index("y_lo")
    ids = jnp.stack([x, zy, (x * 8 + zy) * context.shape[0]]).astype(jnp.int32)
    cut_wide = jnp.broadcast_to(cutoff[:, None], (cutoff.shape[0], HEAD_DIM))

    own = project_queries(latent_in, wq_cross)
    keys = project_context(context, wk_cross, "keys")
    other = moved(own, "y_lo", 2, 1)
    y_lo = lax.axis_index("y_lo")
    pair = jnp.where(
        y_lo == 0, jnp.concatenate([own, other]), jnp.concatenate([other, own])
    )
    values = project_context(context, wv_cross, "values")
    z = lax.axis_index("z")
    ring = [pair] + [moved(pair, "z", 4, offset) for offset in (1, 2, 3)]
    pieces = [
        lax.dynamic_index_in_dim(jnp.stack(ring), (z - place) % 4, 0, False) for place in range(4)
    ]
    mine = jnp.concatenate(pieces)
    blocks = {0: mine}
    for offset in (1, 2, 3):
        blocks[(4 - offset) % 4] = moved(mine, "x", 4, offset)

    parts = []
    for offset in (0, 2, 1, 3):
        part = cross_attend(offset, ids, cutoff, blocks[offset], keys, values, cut_wide)
        parts.append(moved(part, "x", 4, offset) if offset else part)
    mixed = blend_parts(parts)
    rows = latent_in.shape[0]
    mixed = mixed.reshape(8, rows, mixed.shape[1])
    mixed = lax.all_to_all(mixed, ("z", "y_lo"), 0, 0)
    cross_part = cross_output(mixed, wo_cross)
    one, two = summed_over_tp(cross_part)

    state, *sent = self_project(ids, latent_in, one, two, wq_self, wk_self, wv_self)
    parts = [sent[0]] + [moved(sent[o], "x", 4, o) for o in (1, 2, 3)]
    kv = jnp.concatenate([part[:, HEAD_DIM:] for part in parts])
    kv = lax.all_to_all(jnp.broadcast_to(kv[None], (8,) + kv.shape), ("z", "y_lo"), 0, 0)
    outs = self_attend(ids, parts, kv)
    outs = [outs[0]] + [moved(outs[o], "x", 4, -o) for o in (1, 2, 3)]
    self_part = self_output(ids, outs, wo_self)
    one, two = summed_over_tp(self_part)
    return (state + (one.astype(F32) + two.astype(F32))).astype(BF16)


def solution(mesh):
    fine = Mesh(
        mesh.devices.reshape(4, 4, 2, 2, 2), ("x", "z", "y_lo", "y_hi", "core")
    )
    seq, tp = ("x", "z", "y_lo"), ("y_hi", "core")
    in_specs = (
        P(seq, None),
        P(seq, None),
        P(),
        P(None, tp),
        P(None, tp),
        P(None, tp),
        P(tp, None),
        P(None, tp),
        P(None, tp),
        P(None, tp),
        P(tp, None),
    )
    return jax.shard_map(
        on_device, mesh=fine, in_specs=in_specs, out_specs=P(seq, None), check_vma=False
    )
```

```python
import functools

import jax
import jax.numpy as jnp
from jax import lax
from jax.experimental import pallas as pl
from jax.experimental.pallas import tpu as pltpu
from jax.sharding import Mesh, PartitionSpec as P

HEAD_DIM = 128
EPSILON = 1e-05
MASKED_SCORE = -1e30
LOG2E = 1.4426950408889634
MIB = 1 << 20
F32 = jnp.float32
BF16 = jnp.bfloat16

VMEM = pl.BlockSpec(memory_space=pltpu.VMEM)
SMEM = pl.BlockSpec(memory_space=pltpu.SMEM)


def shape_of(dims, dtype=BF16):
    return jax.ShapeDtypeStruct(dims, dtype)


def params(mib):
    return pltpu.CompilerParams(vmem_limit_bytes=mib * MIB)


def cost(flops, nbytes, trans=0):
    return pl.CostEstimate(flops=flops, bytes_accessed=nbytes, transcendentals=trans)


def dot(a, b):
    return jnp.dot(a, b, preferred_element_type=F32)


def dot_t(a, b):
    return lax.dot_general(a, b, (((1,), (1,)), ((), ())), preferred_element_type=F32)


def inv_rms(tile):
    return lax.rsqrt(jnp.mean(tile * tile, axis=-1, keepdims=True) + EPSILON)


def query_kernel(latent_ref, wq_ref, out_ref):
    tile = latent_ref[...].astype(F32)
    normed = (tile * inv_rms(tile)).astype(BF16)
    factor = HEAD_DIM ** (-0.5) * LOG2E
    out_ref[...] = (dot(normed, wq_ref[...]) * factor).astype(BF16)


def project_queries(latent_in, wq):
    rows, width = latent_in.shape
    cols = wq.shape[1]
    return pl.pallas_call(
        query_kernel,
        out_shape=shape_of((rows, cols)),
        in_specs=[VMEM, VMEM],
        out_specs=VMEM,
        compiler_params=params(8),
        cost_estimate=cost(2 * rows * width * cols, 2 * width * cols),
        name="queries",
    )(latent_in, wq)


def context_kernel(step, context_ref, w_ref, after_ref, out_ref):
    def rows_from(i, _):
        here = pl.ds(pl.multiple_of(i * step, step), step)
        tile = context_ref[here, :]
        out_ref[here, :] = (dot(tile, w_ref[...]) * inv_rms(tile.astype(F32))).astype(BF16)
        return 0

    lax.fori_loop(0, context_ref.shape[0] // step, rows_from, 0)


def project_context(context, weight, after, name):
    rows, width = context.shape
    cols = weight.shape[1]
    return pl.pallas_call(
        functools.partial(context_kernel, min(512, rows)),
        out_shape=shape_of((rows, cols)),
        in_specs=[VMEM, VMEM, pl.BlockSpec(memory_space=pl.ANY)],
        out_specs=VMEM,
        compiler_params=params(20),
        cost_estimate=cost(2 * rows * width * cols, 2 * (rows * width + width * cols)),
        name=name,
    )(context, weight, after)


def packed_totals(totals):
    lane = lax.broadcasted_iota(jnp.int32, totals[0].shape, 1)
    held = jnp.zeros(totals[0].shape, F32)
    for head, total in enumerate(totals):
        held = jnp.where(lane == head, total, held)
    high = held.astype(BF16).astype(F32)
    rest = held - high
    mid = rest.astype(BF16).astype(F32)
    low = rest - mid
    return (high + pltpu.roll(mid, 4, 1) + pltpu.roll(low, 8, 1)).astype(BF16)


def spread_matrix(heads):
    dims = (HEAD_DIM, heads * HEAD_DIM)
    row = lax.broadcasted_iota(jnp.int32, dims, 0)
    head = lax.broadcasted_iota(jnp.int32, dims, 1) >> 7
    return jnp.where((row < 12) & ((row & 3) == head), 1.0, 0.0).astype(BF16)


def cross_kernel(offset, ids_ref, cutoff_ref, q_ref, k_ref, v_ref, cut_ref, out_ref, bias):
    rows, cols = q_ref.shape
    heads = cols // HEAD_DIM
    places = k_ref.shape[0]
    step = 512
    block = lax.rem(ids_ref[0] + offset, 4)
    start = block * rows
    first_pos = ids_ref[2]
    lowest = cutoff_ref[start] - first_pos
    highest = cutoff_ref[start + rows - 1] - first_pos
    spans = [slice(head * HEAD_DIM, (head + 1) * HEAD_DIM) for head in range(heads)]

    @pl.when(highest < 0)
    def _():
        out_ref[:, :cols] = jnp.zeros((rows, cols), BF16)
        out_ref[:, cols:] = packed_totals(
            [jnp.full((rows, HEAD_DIM), MASKED_SCORE, F32)] * heads
        )

    def attend(masked):
        ones = jnp.ones((step, HEAD_DIM), BF16)
        if masked:
            cut = cut_ref[pl.ds(pl.multiple_of(start, rows), rows), :] - first_pos
            order = lax.broadcasted_iota(jnp.int32, (rows, HEAD_DIM), 1)
            for place in range(0, places, HEAD_DIM):
                bias[:, place : place + HEAD_DIM] = jnp.where(
                    order + place <= cut, 0.0, MASKED_SCORE
                )

        def scores_of(head):
            scores = dot_t(q_ref[:, spans[head]], k_ref[:, spans[head]])
            return scores + bias[...] if masked else scores

        totals = []
        scores = scores_of(0)
        for head in range(heads):
            peak = jnp.max(scores, axis=1, keepdims=True)
            later = scores_of(head + 1) if head + 1 < heads else None
            both = jnp.zeros((rows, 2 * HEAD_DIM), F32)
            for place in range(0, places, step):
                here = slice(place, place + step)
                probs = jnp.exp2(scores[:, here] - peak).astype(BF16)
                both += dot(probs, jnp.concatenate([v_ref[here, spans[head]], ones], axis=1))
            total = both[:, HEAD_DIM:]
            out_ref[:, spans[head]] = (both[:, :HEAD_DIM] / total).astype(BF16)
            whole = jnp.log2(total) + peak
            totals.append(jnp.where(cut >= 0, whole, MASKED_SCORE) if masked else whole)
            scores = later
        out_ref[:, cols:] = packed_totals(totals)

    @pl.when((highest >= 0) & (lowest < places - 1))
    def _():
        attend(True)

    @pl.when(lowest >= places - 1)
    def _():
        attend(False)


def cross_attend(offset, ids, cutoff, queries, keys, values, cut_wide):
    rows, cols = queries.shape
    places = keys.shape[0]
    return pl.pallas_call(
        functools.partial(cross_kernel, offset),
        out_shape=shape_of((rows, cols + HEAD_DIM)),
        in_specs=[SMEM, SMEM, VMEM, VMEM, VMEM, VMEM],
        out_specs=VMEM,
        scratch_shapes=[pltpu.VMEM((rows, places), F32)],
        compiler_params=params(20),
        cost_estimate=cost(8 * rows * places * cols, 4 * places * cols, rows * places * 4),
        name="cross",
    )(ids, cutoff, queries, keys, values, cut_wide)


def blend(parts, spread, heads):
    cols = heads * HEAD_DIM
    totals = [dot(part[:, cols:], spread) for part in parts]
    peak = functools.reduce(jnp.maximum, totals)
    weights = [jnp.exp2(total - peak) for total in totals]
    weight_sum = functools.reduce(jnp.add, weights)
    mixed = functools.reduce(
        jnp.add, [w * part[:, :cols].astype(F32) for w, part in zip(weights, parts)]
    )
    return mixed / weight_sum, peak + jnp.log2(weight_sum)


def blend_kernel(a_ref, b_ref, c_ref, d_ref, out_ref):
    rows, width = a_ref.shape
    heads = width // HEAD_DIM - 1
    cols = heads * HEAD_DIM
    mixed, whole = blend(
        [a_ref[...], b_ref[...], c_ref[...], d_ref[...]], spread_matrix(heads), heads
    )
    out_ref[:, :cols] = mixed.astype(BF16)
    out_ref[:, cols:] = packed_totals(
        [whole[:, head * HEAD_DIM : (head + 1) * HEAD_DIM] for head in range(heads)]
    )


def blend_parts(parts):
    return pl.pallas_call(
        blend_kernel,
        out_shape=shape_of(parts[0].shape),
        in_specs=[VMEM] * 4,
        out_specs=VMEM,
        compiler_params=params(16),
        name="blend",
    )(*parts)


def cross_output_kernel(parts_ref, wo_ref, out_ref):
    heads = parts_ref.shape[2] // HEAD_DIM - 1
    parts = [parts_ref[i] for i in range(parts_ref.shape[0])]
    mixed, _ = blend(parts, spread_matrix(heads), heads)
    out_ref[...] = dot(mixed.astype(BF16), wo_ref[...]).astype(BF16)


def cross_output(parts, wo):
    return pl.pallas_call(
        cross_output_kernel,
        out_shape=shape_of((parts.shape[1], wo.shape[1])),
        in_specs=[VMEM] * 2,
        out_specs=VMEM,
        compiler_params=params(16),
        name="cross_output",
    )(parts, wo)


def self_project_kernel(
    ids_ref, latent_ref, one_ref, two_ref, wq_ref, wk_ref, wv_ref, state_ref, *rest
):
    outs, held = rest[:4], rest[4]
    rows, cols = held.shape[1:]
    state = latent_ref[...].astype(F32) + (one_ref[...].astype(F32) + two_ref[...].astype(F32))
    state_ref[...] = state
    normed = (state * inv_rms(state)).astype(BF16)
    held[0] = (dot(normed, wq_ref[...]) * (HEAD_DIM ** (-0.5) * LOG2E)).astype(BF16)
    held[1] = dot(normed, wk_ref[...]).astype(BF16)
    held[2] = dot(normed, wv_ref[...]).astype(BF16)
    for offset in range(4):
        head = lax.rem(ids_ref[0] + offset, 4)
        span = pl.ds(pl.multiple_of(head * HEAD_DIM, HEAD_DIM), HEAD_DIM)
        for part in range(3):
            outs[offset][:, part * HEAD_DIM : (part + 1) * HEAD_DIM] = held[part, :, span]


def self_project(ids, latent_in, one, two, wq, wk, wv):
    rows, width = latent_in.shape
    return pl.pallas_call(
        self_project_kernel,
        out_shape=[shape_of((rows, width), F32)] + [shape_of((rows, 3 * HEAD_DIM))] * 4,
        in_specs=[SMEM] + [VMEM] * 6,
        out_specs=[VMEM] * 5,
        scratch_shapes=[pltpu.VMEM((3, rows, wq.shape[1]), BF16)],
        compiler_params=params(24),
        name="self_project",
    )(ids, latent_in, one, two, wq, wk, wv)


def self_kernel(ids_ref, a_ref, b_ref, c_ref, d_ref, kv_ref, *outs):
    rows = a_ref.shape[0]
    groups, group_rows, _ = kv_ref.shape
    own_x, own_zy = ids_ref[0], ids_ref[1]
    q = jnp.concatenate([ref[:, :HEAD_DIM] for ref in (a_ref, b_ref, c_ref, d_ref)], axis=0)
    k = jnp.concatenate([kv_ref[i, :, :HEAD_DIM] for i in range(groups)], axis=0)
    v = jnp.concatenate([kv_ref[i, :, HEAD_DIM:] for i in range(groups)], axis=0)
    scores = dot_t(q, k)
    q_row = lax.broadcasted_iota(jnp.int32, scores.shape, 0)
    k_row = lax.broadcasted_iota(jnp.int32, scores.shape, 1)
    shift = rows.bit_length() - 1
    q_x = (own_x - (q_row >> shift)) & 3
    q_place = (q_x * groups + own_zy) * rows + (q_row & (rows - 1))
    group = k_row >> (group_rows.bit_length() - 1)
    k_x = (own_x - (k_row >> shift)) & 3
    k_place = (k_x * groups + group) * rows + (k_row & (rows - 1))
    scores = jnp.where(k_place <= q_place, scores, MASKED_SCORE)
    peak = jnp.max(scores, axis=1, keepdims=True)
    probs = jnp.exp2(scores - peak).astype(BF16)
    both = dot(probs, jnp.concatenate([v, jnp.ones(v.shape, BF16)], axis=1))
    result = (both[:, :HEAD_DIM] / both[:, HEAD_DIM:]).astype(BF16)
    for offset in range(4):
        outs[offset][...] = result[offset * rows : (offset + 1) * rows]


def self_attend(ids, parts, kv):
    rows = parts[0].shape[0]
    return pl.pallas_call(
        self_kernel,
        out_shape=[shape_of((rows, HEAD_DIM))] * 4,
        in_specs=[SMEM] + [VMEM] * 5,
        out_specs=[VMEM] * 4,
        compiler_params=params(16),
        name="self_attend",
    )(ids, *parts, kv)


def self_output_kernel(ids_ref, a_ref, b_ref, c_ref, d_ref, wo_ref, out_ref, held):
    for offset, ref in enumerate((a_ref, b_ref, c_ref, d_ref)):
        head = lax.rem(ids_ref[0] + offset, 4)
        held[:, pl.ds(pl.multiple_of(head * HEAD_DIM, HEAD_DIM), HEAD_DIM)] = ref[...]
    out_ref[...] = dot(held[...], wo_ref[...]).astype(BF16)


def self_output(ids, parts, wo):
    rows = parts[0].shape[0]
    return pl.pallas_call(
        self_output_kernel,
        out_shape=shape_of((rows, wo.shape[1])),
        in_specs=[SMEM] + [VMEM] * 5,
        out_specs=VMEM,
        scratch_shapes=[pltpu.VMEM((rows, wo.shape[0]), BF16)],
        compiler_params=params(16),
        name="self_output",
    )(ids, *parts, wo)


def moved(tensor, axis, size, offset):
    return lax.ppermute(tensor, axis, [(i, (i + offset) % size) for i in range(size)])


def summed_over_tp(part):
    other = moved(part, "core", 2, 1)
    pair = (part.astype(F32) + other.astype(F32)).astype(BF16)
    return pair, moved(pair, "y_hi", 2, 1)


def on_device(
    context,
    latent_in,
    cutoff,
    wq_cross,
    wk_cross,
    wv_cross,
    wo_cross,
    wq_self,
    wk_self,
    wv_self,
    wo_self,
):
    x = lax.axis_index("x")
    zy = lax.axis_index("z") * 2 + lax.axis_index("y_lo")
    ids = jnp.stack([x, zy, (x * 8 + zy) * context.shape[0]]).astype(jnp.int32)
    cut_wide = jnp.broadcast_to(cutoff[:, None], (cutoff.shape[0], HEAD_DIM))

    own = project_queries(latent_in, wq_cross)
    other = moved(own, "y_lo", 2, 1)
    y_lo = lax.axis_index("y_lo")
    pair = jnp.where(
        y_lo == 0, jnp.concatenate([own, other]), jnp.concatenate([other, own])
    )
    keys = project_context(context, wk_cross, pair, "keys")
    z = lax.axis_index("z")
    ring = [pair] + [moved(pair, "z", 4, offset) for offset in (1, 2, 3)]
    pieces = [
        lax.dynamic_index_in_dim(jnp.stack(ring), (z - place) % 4, 0, False) for place in range(4)
    ]
    mine = jnp.concatenate(pieces)
    values = project_context(context, wv_cross, mine, "values")
    blocks = {0: mine}
    for offset in (2, 3, 1):
        blocks[(4 - offset) % 4] = moved(mine, "x", 4, offset)

    parts = []
    for offset in (0, 1, 2, 3):
        part = cross_attend(offset, ids, cutoff, blocks[offset], keys, values, cut_wide)
        parts.append(moved(part, "x", 4, offset) if offset else part)
    mixed = blend_parts(parts)
    rows = latent_in.shape[0]
    mixed = mixed.reshape(8, rows, mixed.shape[1])
    mixed = lax.all_to_all(mixed, ("z", "y_lo"), 0, 0)
    cross_part = cross_output(mixed, wo_cross)
    one, two = summed_over_tp(cross_part)

    state, *sent = self_project(ids, latent_in, one, two, wq_self, wk_self, wv_self)
    parts = [sent[0]] + [moved(sent[o], "x", 4, o) for o in (1, 2, 3)]
    kv = jnp.concatenate([part[:, HEAD_DIM:] for part in parts])
    kv = lax.all_to_all(jnp.broadcast_to(kv[None], (8,) + kv.shape), ("z", "y_lo"), 0, 0)
    outs = self_attend(ids, parts, kv)
    outs = [outs[0]] + [moved(outs[o], "x", 4, -o) for o in (1, 2, 3)]
    self_part = self_output(ids, outs, wo_self)
    one, two = summed_over_tp(self_part)
    return (state + (one.astype(F32) + two.astype(F32))).astype(BF16)


def solution(mesh):
    fine = Mesh(
        mesh.devices.reshape(4, 4, 2, 2, 2), ("x", "z", "y_lo", "y_hi", "core")
    )
    seq, tp = ("x", "z", "y_lo"), ("y_hi", "core")
    in_specs = (
        P(seq, None),
        P(seq, None),
        P(),
        P(None, tp),
        P(None, tp),
        P(None, tp),
        P(tp, None),
        P(None, tp),
        P(None, tp),
        P(None, tp),
        P(tp, None),
    )
    return jax.shard_map(
        on_device, mesh=fine, in_specs=in_specs, out_specs=P(seq, None), check_vma=False
    )
```

```python
import functools

import jax
import jax.numpy as jnp
import numpy as np
from jax import lax
from jax.experimental import pallas as pl
from jax.experimental.pallas import tpu as pltpu
from jax.sharding import Mesh, PartitionSpec as P

HEAD_DIM = 128
EPSILON = 1e-05
MASKED_SCORE = -1e30
LOG2E = 1.4426950408889634
MIB = 1 << 20
F32 = jnp.float32
BF16 = jnp.bfloat16

VMEM = pl.BlockSpec(memory_space=pltpu.VMEM)
SMEM = pl.BlockSpec(memory_space=pltpu.SMEM)


def shape_of(dims, dtype=BF16):
    return jax.ShapeDtypeStruct(dims, dtype)


def params(mib):
    return pltpu.CompilerParams(vmem_limit_bytes=mib * MIB)


def cost(flops, nbytes, trans=0):
    return pl.CostEstimate(flops=flops, bytes_accessed=nbytes, transcendentals=trans)


def dot(a, b):
    return jnp.dot(a, b, preferred_element_type=F32)


def dot_t(a, b):
    return lax.dot_general(a, b, (((1,), (1,)), ((), ())), preferred_element_type=F32)


def inv_rms(tile):
    return lax.rsqrt(jnp.mean(tile * tile, axis=-1, keepdims=True) + EPSILON)


def query_kernel(latent_ref, wq_ref, out_ref):
    tile = latent_ref[...].astype(F32)
    normed = (tile * inv_rms(tile)).astype(BF16)
    factor = HEAD_DIM ** (-0.5) * LOG2E
    out_ref[...] = (dot(normed, wq_ref[...]) * factor).astype(BF16)


def project_queries(latent_in, wq):
    rows, width = latent_in.shape
    cols = wq.shape[1]
    return pl.pallas_call(
        query_kernel,
        out_shape=shape_of((rows, cols)),
        in_specs=[VMEM, VMEM],
        out_specs=VMEM,
        compiler_params=params(8),
        cost_estimate=cost(2 * rows * width * cols, 2 * width * cols),
        name="queries",
    )(latent_in, wq)


def context_kernel(step, context_ref, w_ref, after_ref, out_ref):
    def rows_from(i, _):
        here = pl.ds(pl.multiple_of(i * step, step), step)
        tile = context_ref[here, :]
        out_ref[here, :] = (dot(tile, w_ref[...]) * inv_rms(tile.astype(F32))).astype(BF16)
        return 0

    lax.fori_loop(0, context_ref.shape[0] // step, rows_from, 0)


def project_context(context, weight, after, name):
    rows, width = context.shape
    cols = weight.shape[1]
    return pl.pallas_call(
        functools.partial(context_kernel, min(512, rows)),
        out_shape=shape_of((rows, cols)),
        in_specs=[VMEM, VMEM, pl.BlockSpec(memory_space=pl.ANY)],
        out_specs=VMEM,
        compiler_params=params(20),
        cost_estimate=cost(2 * rows * width * cols, 2 * (rows * width + width * cols)),
        name=name,
    )(context, weight, after)


def packed_totals(totals):
    lane = lax.broadcasted_iota(jnp.int32, totals[0].shape, 1)
    held = jnp.zeros(totals[0].shape, F32)
    for head, total in enumerate(totals):
        held = jnp.where(lane == head, total, held)
    high = held.astype(BF16).astype(F32)
    rest = held - high
    mid = rest.astype(BF16).astype(F32)
    low = rest - mid
    return (high + pltpu.roll(mid, 4, 1) + pltpu.roll(low, 8, 1)).astype(BF16)


def spread_matrix(heads):
    dims = (HEAD_DIM, heads * HEAD_DIM)
    row = lax.broadcasted_iota(jnp.int32, dims, 0)
    head = lax.broadcasted_iota(jnp.int32, dims, 1) >> 7
    return jnp.where((row < 12) & ((row & 3) == head), 1.0, 0.0).astype(BF16)


def cross_kernel(offset, ids_ref, cutoff_ref, q_ref, k_ref, v_ref, cut_ref, out_ref, bias):
    rows, cols = q_ref.shape
    heads = cols // HEAD_DIM
    places = k_ref.shape[0]
    step = 512
    block = lax.rem(ids_ref[0] + offset, 4)
    start = block * rows
    first_pos = ids_ref[2]
    lowest = cutoff_ref[start] - first_pos
    highest = cutoff_ref[start + rows - 1] - first_pos
    spans = [slice(head * HEAD_DIM, (head + 1) * HEAD_DIM) for head in range(heads)]

    @pl.when(highest < 0)
    def _():
        out_ref[:, :cols] = jnp.zeros((rows, cols), BF16)
        out_ref[:, cols:] = packed_totals(
            [jnp.full((rows, HEAD_DIM), MASKED_SCORE, F32)] * heads
        )

    def attend(masked):
        ones = jnp.ones((step, HEAD_DIM), BF16)
        if masked:
            cut = cut_ref[pl.ds(pl.multiple_of(start, rows), rows), :] - first_pos
            order = lax.broadcasted_iota(jnp.int32, (rows, HEAD_DIM), 1)
            for place in range(0, places, HEAD_DIM):
                bias[:, place : place + HEAD_DIM] = jnp.where(
                    order + place <= cut, 0.0, MASKED_SCORE
                )

        def scores_of(head):
            scores = dot_t(q_ref[:, spans[head]], k_ref[:, spans[head]])
            return scores + bias[...] if masked else scores

        totals = []
        scores = scores_of(0)
        for head in range(heads):
            peak = jnp.max(scores, axis=1, keepdims=True)
            later = scores_of(head + 1) if head + 1 < heads else None
            both = jnp.zeros((rows, 2 * HEAD_DIM), F32)
            for place in range(0, places, step):
                here = slice(place, place + step)
                probs = jnp.exp2(scores[:, here] - peak).astype(BF16)
                both += dot(probs, jnp.concatenate([v_ref[here, spans[head]], ones], axis=1))
            total = both[:, HEAD_DIM:]
            out_ref[:, spans[head]] = (both[:, :HEAD_DIM] / total).astype(BF16)
            whole = jnp.log2(total) + peak
            totals.append(jnp.where(cut >= 0, whole, MASKED_SCORE) if masked else whole)
            scores = later
        out_ref[:, cols:] = packed_totals(totals)

    @pl.when((highest >= 0) & (lowest < places - 1))
    def _():
        attend(True)

    @pl.when(lowest >= places - 1)
    def _():
        attend(False)


def cross_attend(offset, ids, cutoff, queries, keys, values, cut_wide):
    rows, cols = queries.shape
    places = keys.shape[0]
    return pl.pallas_call(
        functools.partial(cross_kernel, offset),
        out_shape=shape_of((rows, cols + HEAD_DIM)),
        in_specs=[SMEM, SMEM, VMEM, VMEM, VMEM, VMEM],
        out_specs=VMEM,
        scratch_shapes=[pltpu.VMEM((rows, places), F32)],
        compiler_params=params(20),
        cost_estimate=cost(8 * rows * places * cols, 4 * places * cols, rows * places * 4),
        name="cross",
    )(ids, cutoff, queries, keys, values, cut_wide)


def blend(parts, spread, heads):
    cols = heads * HEAD_DIM
    totals = [dot(part[:, cols:], spread) for part in parts]
    peak = functools.reduce(jnp.maximum, totals)
    weights = [jnp.exp2(total - peak) for total in totals]
    weight_sum = functools.reduce(jnp.add, weights)
    mixed = functools.reduce(
        jnp.add, [w * part[:, :cols].astype(F32) for w, part in zip(weights, parts)]
    )
    return mixed / weight_sum, peak + jnp.log2(weight_sum)


def blend_kernel(a_ref, b_ref, c_ref, d_ref, out_ref):
    rows, width = a_ref.shape
    heads = width // HEAD_DIM - 1
    cols = heads * HEAD_DIM
    mixed, whole = blend(
        [a_ref[...], b_ref[...], c_ref[...], d_ref[...]], spread_matrix(heads), heads
    )
    out_ref[:, :cols] = mixed.astype(BF16)
    out_ref[:, cols:] = packed_totals(
        [whole[:, head * HEAD_DIM : (head + 1) * HEAD_DIM] for head in range(heads)]
    )


def blend_parts(parts):
    return pl.pallas_call(
        blend_kernel,
        out_shape=shape_of(parts[0].shape),
        in_specs=[VMEM] * 4,
        out_specs=VMEM,
        compiler_params=params(16),
        name="blend",
    )(*parts)


def cross_output_kernel(parts_ref, wo_ref, out_ref):
    heads = parts_ref.shape[2] // HEAD_DIM - 1
    parts = [parts_ref[i] for i in range(parts_ref.shape[0])]
    mixed, _ = blend(parts, spread_matrix(heads), heads)
    out_ref[...] = dot(mixed.astype(BF16), wo_ref[...]).astype(BF16)


def cross_output(parts, wo):
    return pl.pallas_call(
        cross_output_kernel,
        out_shape=shape_of((parts.shape[1], wo.shape[1])),
        in_specs=[VMEM] * 2,
        out_specs=VMEM,
        compiler_params=params(16),
        name="cross_output",
    )(parts, wo)


def self_project_kernel(
    ids_ref, latent_ref, one_ref, two_ref, wq_ref, wk_ref, wv_ref, state_ref, *rest
):
    outs, held = rest[:4], rest[4]
    rows, cols = held.shape[1:]
    state = latent_ref[...].astype(F32) + (one_ref[...].astype(F32) + two_ref[...].astype(F32))
    state_ref[...] = state
    normed = (state * inv_rms(state)).astype(BF16)
    held[0] = (dot(normed, wq_ref[...]) * (HEAD_DIM ** (-0.5) * LOG2E)).astype(BF16)
    held[1] = dot(normed, wk_ref[...]).astype(BF16)
    held[2] = dot(normed, wv_ref[...]).astype(BF16)
    for offset in range(4):
        head = lax.rem(ids_ref[0] + offset, 4)
        span = pl.ds(pl.multiple_of(head * HEAD_DIM, HEAD_DIM), HEAD_DIM)
        for part in range(3):
            outs[offset][:, part * HEAD_DIM : (part + 1) * HEAD_DIM] = held[part, :, span]


def self_project(ids, latent_in, one, two, wq, wk, wv):
    rows, width = latent_in.shape
    return pl.pallas_call(
        self_project_kernel,
        out_shape=[shape_of((rows, width), F32)] + [shape_of((rows, 3 * HEAD_DIM))] * 4,
        in_specs=[SMEM] + [VMEM] * 6,
        out_specs=[VMEM] * 5,
        scratch_shapes=[pltpu.VMEM((3, rows, wq.shape[1]), BF16)],
        compiler_params=params(24),
        name="self_project",
    )(ids, latent_in, one, two, wq, wk, wv)


def self_kernel(ids_ref, a_ref, b_ref, c_ref, d_ref, kv_ref, *outs):
    rows = a_ref.shape[0]
    groups, group_rows, _ = kv_ref.shape
    own_a, own_b, stride_a, stride_b, own_y = (ids_ref[i] for i in (0, 1, 3, 4, 5))
    q = jnp.concatenate([ref[:, :HEAD_DIM] for ref in (a_ref, b_ref, c_ref, d_ref)], axis=0)
    k = jnp.concatenate([kv_ref[i, :, :HEAD_DIM] for i in range(groups)], axis=0)
    v = jnp.concatenate([kv_ref[i, :, HEAD_DIM:] for i in range(groups)], axis=0)
    scores = dot_t(q, k)
    q_row = lax.broadcasted_iota(jnp.int32, scores.shape, 0)
    k_row = lax.broadcasted_iota(jnp.int32, scores.shape, 1)
    shift = rows.bit_length() - 1
    q_a = (own_a - (q_row >> shift)) & 3
    q_place = q_a * stride_a + (q_row & (rows - 1)) + (own_b * stride_b + own_y * rows)
    group = k_row >> (group_rows.bit_length() - 1)
    k_a = (own_a - (k_row >> shift)) & 3
    k_place = k_a * stride_a + (group >> 1) * stride_b + (group & 1) * rows + (k_row & (rows - 1))
    scores = jnp.where(k_place <= q_place, scores, MASKED_SCORE)
    peak = jnp.max(scores, axis=1, keepdims=True)
    probs = jnp.exp2(scores - peak).astype(BF16)
    both = dot(probs, jnp.concatenate([v, jnp.ones(v.shape, BF16)], axis=1))
    result = (both[:, :HEAD_DIM] / both[:, HEAD_DIM:]).astype(BF16)
    for offset in range(4):
        outs[offset][...] = result[offset * rows : (offset + 1) * rows]


def self_attend(ids, parts, kv):
    rows = parts[0].shape[0]
    return pl.pallas_call(
        self_kernel,
        out_shape=[shape_of((rows, HEAD_DIM))] * 4,
        in_specs=[SMEM] + [VMEM] * 5,
        out_specs=[VMEM] * 4,
        compiler_params=params(16),
        name="self_attend",
    )(ids, *parts, kv)


def self_output_kernel(ids_ref, a_ref, b_ref, c_ref, d_ref, wo_ref, out_ref, held):
    for offset, ref in enumerate((a_ref, b_ref, c_ref, d_ref)):
        head = lax.rem(ids_ref[0] + offset, 4)
        held[:, pl.ds(pl.multiple_of(head * HEAD_DIM, HEAD_DIM), HEAD_DIM)] = ref[...]
    out_ref[...] = dot(held[...], wo_ref[...]).astype(BF16)


def self_output(ids, parts, wo):
    rows = parts[0].shape[0]
    return pl.pallas_call(
        self_output_kernel,
        out_shape=shape_of((rows, wo.shape[1])),
        in_specs=[SMEM] + [VMEM] * 5,
        out_specs=VMEM,
        scratch_shapes=[pltpu.VMEM((rows, wo.shape[0]), BF16)],
        compiler_params=params(16),
        name="self_output",
    )(ids, *parts, wo)


def moved(tensor, axis, size, offset):
    return lax.ppermute(tensor, axis, [(i, (i + offset) % size) for i in range(size)])


PLANE = ("x", "z", "core")
WHOLE = ("x", "z", "y_lo", "y_hi", "core")


def turned(tensor, axis, offset):
    pairs = []
    for x in range(4):
        for z in range(4):
            for core in range(2):
                if (axis == "a") == (core == 0):
                    to = ((x + offset) % 4, z)
                else:
                    to = (x, (z + offset) % 4)
                pairs.append(((x * 4 + z) * 2 + core, (to[0] * 4 + to[1]) * 2 + core))
    return lax.ppermute(tensor, PLANE, pairs)


def exchanged(tensor):
    order = np.arange(128).reshape(4, 4, 2, 2, 2)
    groups = []
    for y_hi in range(2):
        for a in range(4):
            groups.append(order[a, :, :, y_hi, 0].reshape(-1).tolist())
            groups.append(order[:, a, :, y_hi, 1].reshape(-1).tolist())
    return lax.all_to_all(tensor, WHOLE, 0, 0, axis_index_groups=groups)


def summed_over_tp(part):
    other = moved(part, "core", 2, 1)
    pair = (part.astype(F32) + other.astype(F32)).astype(BF16)
    return pair, moved(pair, "y_hi", 2, 1)


def on_device(
    context,
    latent_in,
    cutoff,
    wq_cross,
    wk_cross,
    wv_cross,
    wo_cross,
    wq_self,
    wk_self,
    wv_self,
    wo_self,
):
    x, z, y_lo = lax.axis_index("x"), lax.axis_index("z"), lax.axis_index("y_lo")
    first_core = lax.axis_index("core") == 0
    a = jnp.where(first_core, x, z)
    b = jnp.where(first_core, z, x)
    rows = latent_in.shape[0]
    stride_a = jnp.where(first_core, 8 * rows, 2 * rows)
    stride_b = jnp.where(first_core, 2 * rows, 8 * rows)
    first_pos = ((x * 4 + z) * 2 + y_lo) * context.shape[0]
    ids = jnp.stack([a, b, first_pos, stride_a, stride_b, y_lo]).astype(jnp.int32)
    turned_cutoff = cutoff.reshape(4, 4, 2 * rows).transpose(1, 0, 2).reshape(-1)
    cutoff = jnp.where(first_core, cutoff, turned_cutoff)
    cut_wide = jnp.broadcast_to(cutoff[:, None], (cutoff.shape[0], HEAD_DIM))

    own = project_queries(latent_in, wq_cross)
    other = moved(own, "y_lo", 2, 1)
    pair = jnp.where(
        y_lo == 0, jnp.concatenate([own, other]), jnp.concatenate([other, own])
    )
    keys = project_context(context, wk_cross, pair, "keys")
    ring = [pair] + [turned(pair, "b", offset) for offset in (1, 2, 3)]
    pieces = [
        lax.dynamic_index_in_dim(jnp.stack(ring), (b - place) & 3, 0, False) for place in range(4)
    ]
    mine = jnp.concatenate(pieces)
    values = project_context(context, wv_cross, mine, "values")
    blocks = {0: mine}
    for offset in (2, 3, 1):
        blocks[(4 - offset) % 4] = turned(mine, "a", offset)

    parts = []
    for offset in (2, 1, 3, 0):
        part = cross_attend(offset, ids, cutoff, blocks[offset], keys, values, cut_wide)
        parts.append(turned(part, "a", offset) if offset else part)
    mixed = blend_parts(parts)
    mixed = mixed.reshape(8, rows, mixed.shape[1])
    mixed = exchanged(mixed)
    cross_part = cross_output(mixed, wo_cross)
    one, two = summed_over_tp(cross_part)

    state, *sent = self_project(ids, latent_in, one, two, wq_self, wk_self, wv_self)
    parts = [sent[0]] + [turned(sent[o], "a", o) for o in (1, 2, 3)]
    kv = jnp.concatenate([part[:, HEAD_DIM:] for part in parts])
    kv = exchanged(jnp.broadcast_to(kv[None], (8,) + kv.shape))
    outs = self_attend(ids, parts, kv)
    outs = [outs[0]] + [turned(outs[o], "a", -o) for o in (1, 2, 3)]
    self_part = self_output(ids, outs, wo_self)
    one, two = summed_over_tp(self_part)
    return (state + (one.astype(F32) + two.astype(F32))).astype(BF16)


def solution(mesh):
    fine = Mesh(
        mesh.devices.reshape(4, 4, 2, 2, 2), ("x", "z", "y_lo", "y_hi", "core")
    )
    seq, tp = ("x", "z", "y_lo"), ("y_hi", "core")
    in_specs = (
        P(seq, None),
        P(seq, None),
        P(),
        P(None, tp),
        P(None, tp),
        P(None, tp),
        P(tp, None),
        P(None, tp),
        P(None, tp),
        P(None, tp),
        P(tp, None),
    )
    return jax.shard_map(
        on_device, mesh=fine, in_specs=in_specs, out_specs=P(seq, None), check_vma=False
    )
```

```python
import functools

import jax
import jax.numpy as jnp
import numpy as np
from jax import lax
from jax.experimental import pallas as pl
from jax.experimental.pallas import tpu as pltpu
from jax.sharding import Mesh, PartitionSpec as P

HEAD_DIM = 128
EPSILON = 1e-05
MASKED_SCORE = -1e30
LOG2E = 1.4426950408889634
MIB = 1 << 20
F32 = jnp.float32
BF16 = jnp.bfloat16

VMEM = pl.BlockSpec(memory_space=pltpu.VMEM)
SMEM = pl.BlockSpec(memory_space=pltpu.SMEM)


def shape_of(dims, dtype=BF16):
    return jax.ShapeDtypeStruct(dims, dtype)


def params(mib):
    return pltpu.CompilerParams(vmem_limit_bytes=mib * MIB)


def cost(flops, nbytes, trans=0):
    return pl.CostEstimate(flops=flops, bytes_accessed=nbytes, transcendentals=trans)


def dot(a, b):
    return jnp.dot(a, b, preferred_element_type=F32)


def dot_t(a, b):
    return lax.dot_general(a, b, (((1,), (1,)), ((), ())), preferred_element_type=F32)


def inv_rms(tile):
    return lax.rsqrt(jnp.mean(tile * tile, axis=-1, keepdims=True) + EPSILON)


def query_kernel(latent_ref, wq_ref, out_ref):
    tile = latent_ref[...].astype(F32)
    normed = (tile * inv_rms(tile)).astype(BF16)
    factor = HEAD_DIM ** (-0.5) * LOG2E
    out_ref[...] = (dot(normed, wq_ref[...]) * factor).astype(BF16)


def project_queries(latent_in, wq):
    rows, width = latent_in.shape
    cols = wq.shape[1]
    return pl.pallas_call(
        query_kernel,
        out_shape=shape_of((rows, cols)),
        in_specs=[VMEM, VMEM],
        out_specs=VMEM,
        compiler_params=params(8),
        cost_estimate=cost(2 * rows * width * cols, 2 * width * cols),
        name="queries",
    )(latent_in, wq)


def context_kernel(first, step, context_ref, w_ref, after_ref, out_ref):
    def rows_from(i, _):
        there = pl.ds(pl.multiple_of(first + i * step, step), step)
        tile = context_ref[there, :]
        product = dot(tile, w_ref[...]) * inv_rms(tile.astype(F32))
        out_ref[pl.ds(pl.multiple_of(i * step, step), step), :] = product.astype(BF16)
        return 0

    lax.fori_loop(0, out_ref.shape[0] // step, rows_from, 0, unroll=True)


def project_context(context, weight, after, name, first, rows):
    width = context.shape[1]
    cols = weight.shape[1]
    return pl.pallas_call(
        functools.partial(context_kernel, first, min(512, rows)),
        out_shape=shape_of((rows, cols)),
        in_specs=[VMEM, VMEM, pl.BlockSpec(memory_space=pl.ANY)],
        out_specs=VMEM,
        compiler_params=params(20),
        cost_estimate=cost(2 * rows * width * cols, 2 * (rows * width + width * cols)),
        name=name,
    )(context, weight, after)


def packed_totals(totals):
    lane = lax.broadcasted_iota(jnp.int32, totals[0].shape, 1)
    held = jnp.zeros(totals[0].shape, F32)
    for head, total in enumerate(totals):
        held = jnp.where(lane == head, total, held)
    high = held.astype(BF16).astype(F32)
    rest = held - high
    mid = rest.astype(BF16).astype(F32)
    low = rest - mid
    return (high + pltpu.roll(mid, 4, 1) + pltpu.roll(low, 8, 1)).astype(BF16)


def spread_matrix(heads):
    dims = (HEAD_DIM, heads * HEAD_DIM)
    row = lax.broadcasted_iota(jnp.int32, dims, 0)
    head = lax.broadcasted_iota(jnp.int32, dims, 1) >> 7
    return jnp.where((row < 12) & ((row & 3) == head), 1.0, 0.0).astype(BF16)


def cross_kernel(offsets, ids_ref, cutoff_ref, cut_ref, k_ref, more_ref, v_ref, *rest):
    blocks = len(offsets)
    q_refs, out_refs, bias = rest[:blocks], rest[blocks : 2 * blocks], rest[2 * blocks]
    rows, cols = q_refs[0].shape
    heads = cols // HEAD_DIM
    places = v_ref.shape[0]
    step = 512
    first_pos = ids_ref[2]
    starts = [((ids_ref[0] + offset) & 3) * rows for offset in offsets]
    lowest = functools.reduce(jnp.minimum, [cutoff_ref[start] for start in starts])
    highest = functools.reduce(jnp.maximum, [cutoff_ref[start + rows - 1] for start in starts])
    lowest, highest = lowest - first_pos, highest - first_pos
    spans = [slice(head * HEAD_DIM, (head + 1) * HEAD_DIM) for head in range(heads)]

    def stacked(pieces):
        return pieces[0] if blocks == 1 else jnp.concatenate(pieces, axis=0)

    def put(span, value):
        for i, out_ref in enumerate(out_refs):
            out_ref[:, span] = value[i * rows : (i + 1) * rows].astype(BF16)

    @pl.when(highest < 0)
    def _():
        put(slice(0, cols), jnp.zeros((blocks * rows, cols), BF16))
        put(
            slice(cols, cols + HEAD_DIM),
            packed_totals([jnp.full((blocks * rows, HEAD_DIM), MASKED_SCORE, F32)] * heads),
        )

    def attend(masked):
        ones = jnp.ones((step, HEAD_DIM), BF16)
        if masked:
            cut = stacked(
                [cut_ref[pl.ds(pl.multiple_of(start, rows), rows), :] for start in starts]
            )
            cut = cut - first_pos
            order = lax.broadcasted_iota(jnp.int32, cut.shape, 1)
            for place in range(0, places, HEAD_DIM):
                bias[:, place : place + HEAD_DIM] = jnp.where(
                    order + place <= cut, 0.0, MASKED_SCORE
                )

        def scores_of(head):
            queries = stacked([q_ref[:, spans[head]] for q_ref in q_refs])
            keys = jnp.concatenate([k_ref[:, spans[head]], more_ref[:, spans[head]]], axis=0)
            scores = dot_t(queries, keys)
            return scores + bias[...] if masked else scores

        totals = []
        scores = scores_of(0)
        for head in range(heads):
            peak = jnp.max(scores, axis=1, keepdims=True)
            later = scores_of(head + 1) if head + 1 < heads else None
            both = jnp.zeros((blocks * rows, 2 * HEAD_DIM), F32)
            for place in range(0, places, step):
                here = slice(place, place + step)
                probs = jnp.exp2(scores[:, here] - peak).astype(BF16)
                both += dot(probs, jnp.concatenate([v_ref[here, spans[head]], ones], axis=1))
            total = both[:, HEAD_DIM:]
            put(spans[head], both[:, :HEAD_DIM] / total)
            whole = jnp.log2(total) + peak
            totals.append(jnp.where(cut >= 0, whole, MASKED_SCORE) if masked else whole)
            scores = later
        put(slice(cols, cols + HEAD_DIM), packed_totals(totals))

    @pl.when((highest >= 0) & (lowest < places - 1))
    def _():
        attend(True)

    @pl.when(lowest >= places - 1)
    def _():
        attend(False)


def cross_attend(offsets, ids, cutoff, queries, keys, values, cut_wide):
    blocks = len(offsets)
    rows, cols = queries[0].shape
    places = values.shape[0]
    return pl.pallas_call(
        functools.partial(cross_kernel, offsets),
        out_shape=[shape_of((rows, cols + HEAD_DIM))] * blocks,
        in_specs=[SMEM, SMEM] + [VMEM] * (4 + blocks),
        out_specs=[VMEM] * blocks,
        scratch_shapes=[pltpu.VMEM((blocks * rows, places), F32)],
        compiler_params=params(20 if blocks == 1 else 32),
        cost_estimate=cost(
            blocks * 8 * rows * places * cols, 4 * places * cols, blocks * rows * places * 4
        ),
        name="cross",
    )(ids, cutoff, cut_wide, *keys, values, *queries)


def blend(parts, spread, heads):
    cols = heads * HEAD_DIM
    totals = [dot(part[:, cols:], spread) for part in parts]
    peak = functools.reduce(jnp.maximum, totals)
    weights = [jnp.exp2(total - peak) for total in totals]
    weight_sum = functools.reduce(jnp.add, weights)
    mixed = functools.reduce(
        jnp.add, [w * part[:, :cols].astype(F32) for w, part in zip(weights, parts)]
    )
    return mixed / weight_sum, peak + jnp.log2(weight_sum)


def blend_kernel(a_ref, b_ref, c_ref, d_ref, out_ref):
    rows, width = a_ref.shape
    heads = width // HEAD_DIM - 1
    cols = heads * HEAD_DIM
    mixed, whole = blend(
        [a_ref[...], b_ref[...], c_ref[...], d_ref[...]], spread_matrix(heads), heads
    )
    out_ref[:, :cols] = mixed.astype(BF16)
    out_ref[:, cols:] = packed_totals(
        [whole[:, head * HEAD_DIM : (head + 1) * HEAD_DIM] for head in range(heads)]
    )


def blend_parts(parts):
    return pl.pallas_call(
        blend_kernel,
        out_shape=shape_of(parts[0].shape),
        in_specs=[VMEM] * 4,
        out_specs=VMEM,
        compiler_params=params(16),
        name="blend",
    )(*parts)


def cross_output_kernel(parts_ref, wo_ref, out_ref):
    heads = parts_ref.shape[2] // HEAD_DIM - 1
    parts = [parts_ref[i] for i in range(parts_ref.shape[0])]
    mixed, _ = blend(parts, spread_matrix(heads), heads)
    out_ref[...] = dot(mixed.astype(BF16), wo_ref[...]).astype(BF16)


def cross_output(parts, wo):
    return pl.pallas_call(
        cross_output_kernel,
        out_shape=shape_of((parts.shape[1], wo.shape[1])),
        in_specs=[VMEM] * 2,
        out_specs=VMEM,
        compiler_params=params(16),
        name="cross_output",
    )(parts, wo)


def self_project_kernel(
    ids_ref, latent_ref, one_ref, two_ref, wq_ref, wk_ref, wv_ref, state_ref, *rest
):
    outs, held = rest[:4], rest[4]
    rows, cols = held.shape[1:]
    state = latent_ref[...].astype(F32) + (one_ref[...].astype(F32) + two_ref[...].astype(F32))
    state_ref[...] = state
    normed = (state * inv_rms(state)).astype(BF16)
    held[0] = (dot(normed, wq_ref[...]) * (HEAD_DIM ** (-0.5) * LOG2E)).astype(BF16)
    held[1] = dot(normed, wk_ref[...]).astype(BF16)
    held[2] = dot(normed, wv_ref[...]).astype(BF16)
    for offset in range(4):
        head = lax.rem(ids_ref[0] + offset, 4)
        span = pl.ds(pl.multiple_of(head * HEAD_DIM, HEAD_DIM), HEAD_DIM)
        for part in range(3):
            outs[offset][:, part * HEAD_DIM : (part + 1) * HEAD_DIM] = held[part, :, span]


def self_project(ids, latent_in, one, two, wq, wk, wv):
    rows, width = latent_in.shape
    return pl.pallas_call(
        self_project_kernel,
        out_shape=[shape_of((rows, width), F32)] + [shape_of((rows, 3 * HEAD_DIM))] * 4,
        in_specs=[SMEM] + [VMEM] * 6,
        out_specs=[VMEM] * 5,
        scratch_shapes=[pltpu.VMEM((3, rows, wq.shape[1]), BF16)],
        compiler_params=params(24),
        name="self_project",
    )(ids, latent_in, one, two, wq, wk, wv)


def self_kernel(ids_ref, a_ref, b_ref, c_ref, d_ref, kv_ref, *outs):
    rows = a_ref.shape[0]
    groups, group_rows, _ = kv_ref.shape
    own_a, own_b, stride_a, stride_b, own_y = (ids_ref[i] for i in (0, 1, 3, 4, 5))
    q = jnp.concatenate([ref[:, :HEAD_DIM] for ref in (a_ref, b_ref, c_ref, d_ref)], axis=0)
    k = jnp.concatenate([kv_ref[i, :, :HEAD_DIM] for i in range(groups)], axis=0)
    v = jnp.concatenate([kv_ref[i, :, HEAD_DIM:] for i in range(groups)], axis=0)
    scores = dot_t(q, k)
    q_row = lax.broadcasted_iota(jnp.int32, scores.shape, 0)
    k_row = lax.broadcasted_iota(jnp.int32, scores.shape, 1)
    shift = rows.bit_length() - 1
    q_a = (own_a - (q_row >> shift)) & 3
    q_place = q_a * stride_a + (q_row & (rows - 1)) + (own_b * stride_b + own_y * rows)
    group = k_row >> (group_rows.bit_length() - 1)
    k_a = (own_a - (k_row >> shift)) & 3
    k_place = k_a * stride_a + (group >> 1) * stride_b + (group & 1) * rows + (k_row & (rows - 1))
    scores = jnp.where(k_place <= q_place, scores, MASKED_SCORE)
    peak = jnp.max(scores, axis=1, keepdims=True)
    probs = jnp.exp2(scores - peak).astype(BF16)
    both = dot(probs, jnp.concatenate([v, jnp.ones(v.shape, BF16)], axis=1))
    result = (both[:, :HEAD_DIM] / both[:, HEAD_DIM:]).astype(BF16)
    for offset in range(4):
        outs[offset][...] = result[offset * rows : (offset + 1) * rows]


def self_attend(ids, parts, kv):
    rows = parts[0].shape[0]
    return pl.pallas_call(
        self_kernel,
        out_shape=[shape_of((rows, HEAD_DIM))] * 4,
        in_specs=[SMEM] + [VMEM] * 5,
        out_specs=[VMEM] * 4,
        compiler_params=params(16),
        name="self_attend",
    )(ids, *parts, kv)


def self_output_kernel(ids_ref, a_ref, b_ref, c_ref, d_ref, wo_ref, out_ref, held):
    for offset, ref in enumerate((a_ref, b_ref, c_ref, d_ref)):
        head = lax.rem(ids_ref[0] + offset, 4)
        held[:, pl.ds(pl.multiple_of(head * HEAD_DIM, HEAD_DIM), HEAD_DIM)] = ref[...]
    out_ref[...] = dot(held[...], wo_ref[...]).astype(BF16)


def self_output(ids, parts, wo):
    rows = parts[0].shape[0]
    return pl.pallas_call(
        self_output_kernel,
        out_shape=shape_of((rows, wo.shape[1])),
        in_specs=[SMEM] + [VMEM] * 5,
        out_specs=VMEM,
        scratch_shapes=[pltpu.VMEM((rows, wo.shape[0]), BF16)],
        compiler_params=params(16),
        name="self_output",
    )(ids, *parts, wo)


def moved(tensor, axis, size, offset):
    return lax.ppermute(tensor, axis, [(i, (i + offset) % size) for i in range(size)])


PLANE = ("x", "z", "core")
WHOLE = ("x", "z", "y_lo", "y_hi", "core")


def turned(tensor, axis, offset):
    pairs = []
    for x in range(4):
        for z in range(4):
            for core in range(2):
                if (axis == "a") == (core == 0):
                    to = ((x + offset) % 4, z)
                else:
                    to = (x, (z + offset) % 4)
                pairs.append(((x * 4 + z) * 2 + core, (to[0] * 4 + to[1]) * 2 + core))
    return lax.ppermute(tensor, PLANE, pairs)


def exchanged(tensor):
    order = np.arange(128).reshape(4, 4, 2, 2, 2)
    groups = []
    for y_hi in range(2):
        for a in range(4):
            groups.append(order[a, :, :, y_hi, 0].reshape(-1).tolist())
            groups.append(order[:, a, :, y_hi, 1].reshape(-1).tolist())
    return lax.all_to_all(tensor, WHOLE, 0, 0, axis_index_groups=groups)


def summed_over_tp(part):
    other = moved(part, "core", 2, 1)
    pair = (part.astype(F32) + other.astype(F32)).astype(BF16)
    return pair, moved(pair, "y_hi", 2, 1)


def on_device(
    context,
    latent_in,
    cutoff,
    wq_cross,
    wk_cross,
    wv_cross,
    wo_cross,
    wq_self,
    wk_self,
    wv_self,
    wo_self,
):
    x, z, y_lo = lax.axis_index("x"), lax.axis_index("z"), lax.axis_index("y_lo")
    first_core = lax.axis_index("core") == 0
    a = jnp.where(first_core, x, z)
    b = jnp.where(first_core, z, x)
    rows = latent_in.shape[0]
    stride_a = jnp.where(first_core, 8 * rows, 2 * rows)
    stride_b = jnp.where(first_core, 2 * rows, 8 * rows)
    first_pos = ((x * 4 + z) * 2 + y_lo) * context.shape[0]
    ids = jnp.stack([a, b, first_pos, stride_a, stride_b, y_lo]).astype(jnp.int32)
    turned_cutoff = cutoff.reshape(4, 4, 2 * rows).transpose(1, 0, 2).reshape(-1)
    cutoff = jnp.where(first_core, cutoff, turned_cutoff)
    cut_wide = jnp.broadcast_to(cutoff[:, None], (cutoff.shape[0], HEAD_DIM))

    own = project_queries(latent_in, wq_cross)
    other = moved(own, "y_lo", 2, 1)
    pair = jnp.where(
        y_lo == 0, jnp.concatenate([own, other]), jnp.concatenate([other, own])
    )
    half = context.shape[0] // 2
    keys = [project_context(context, wk_cross, pair, "keys", 0, half)]
    came = {offset: turned(pair, "b", offset) for offset in (2, 1, 3)}
    ring = [pair] + [came[offset] for offset in (1, 2, 3)]
    pieces = [
        lax.dynamic_index_in_dim(jnp.stack(ring), (b - place) & 3, 0, False) for place in range(4)
    ]
    mine = jnp.concatenate(pieces)
    keys.append(project_context(context, wk_cross, mine, "keys", half, half))
    values = project_context(context, wv_cross, mine, "values", 0, 2 * half)
    blocks = {0: mine}
    for offset in (2, 3, 1):
        blocks[(4 - offset) % 4] = turned(mine, "a", offset)

    parts = []
    for offsets in ((2, 1), (3,), (0,)):
        queries = [blocks[offset] for offset in offsets]
        made = cross_attend(offsets, ids, cutoff, queries, keys, values, cut_wide)
        for offset, part in zip(offsets, made):
            parts.append(turned(part, "a", offset) if offset else part)
    mixed = blend_parts(parts)
    mixed = mixed.reshape(8, rows, mixed.shape[1])
    mixed = exchanged(mixed)
    cross_part = cross_output(mixed, wo_cross)
    one, two = summed_over_tp(cross_part)

    state, *sent = self_project(ids, latent_in, one, two, wq_self, wk_self, wv_self)
    came = {o: turned(sent[o], "a", o) for o in (2, 1, 3)}
    parts = [sent[0]] + [came[o] for o in (1, 2, 3)]
    kv = jnp.concatenate([part[:, HEAD_DIM:] for part in parts])
    kv = exchanged(jnp.broadcast_to(kv[None], (8,) + kv.shape))
    outs = self_attend(ids, parts, kv)
    came = {o: turned(outs[o], "a", -o) for o in (2, 1, 3)}
    outs = [outs[0]] + [came[o] for o in (1, 2, 3)]
    self_part = self_output(ids, outs, wo_self)
    one, two = summed_over_tp(self_part)
    return (state + (one.astype(F32) + two.astype(F32))).astype(BF16)


def solution(mesh):
    fine = Mesh(
        mesh.devices.reshape(4, 4, 2, 2, 2), ("x", "z", "y_lo", "y_hi", "core")
    )
    seq, tp = ("x", "z", "y_lo"), ("y_hi", "core")
    in_specs = (
        P(seq, None),
        P(seq, None),
        P(),
        P(None, tp),
        P(None, tp),
        P(None, tp),
        P(tp, None),
        P(None, tp),
        P(None, tp),
        P(None, tp),
        P(tp, None),
    )
    return jax.shard_map(
        on_device, mesh=fine, in_specs=in_specs, out_specs=P(seq, None), check_vma=False
    )
```

```python
import functools

import jax
import jax.numpy as jnp
import numpy as np
from jax import lax
from jax.experimental import pallas as pl
from jax.experimental.pallas import tpu as pltpu
from jax.sharding import Mesh, PartitionSpec as P

HEAD_DIM = 128
EPSILON = 1e-05
MASKED_SCORE = -1e30
LOG2E = 1.4426950408889634
MIB = 1 << 20
F32 = jnp.float32
BF16 = jnp.bfloat16

VMEM = pl.BlockSpec(memory_space=pltpu.VMEM)
SMEM = pl.BlockSpec(memory_space=pltpu.SMEM)


def shape_of(dims, dtype=BF16):
    return jax.ShapeDtypeStruct(dims, dtype)


def params(mib):
    return pltpu.CompilerParams(vmem_limit_bytes=mib * MIB)


def cost(flops, nbytes, trans=0):
    return pl.CostEstimate(flops=flops, bytes_accessed=nbytes, transcendentals=trans)


def dot(a, b):
    return jnp.dot(a, b, preferred_element_type=F32)


def dot_t(a, b):
    return lax.dot_general(a, b, (((1,), (1,)), ((), ())), preferred_element_type=F32)


def inv_rms(tile):
    return lax.rsqrt(jnp.mean(tile * tile, axis=-1, keepdims=True) + EPSILON)


def query_kernel(latent_ref, wq_ref, out_ref):
    tile = latent_ref[...].astype(F32)
    normed = (tile * inv_rms(tile)).astype(BF16)
    factor = HEAD_DIM ** (-0.5) * LOG2E
    out_ref[...] = (dot(normed, wq_ref[...]) * factor).astype(BF16)


def project_queries(latent_in, wq):
    rows, width = latent_in.shape
    cols = wq.shape[1]
    return pl.pallas_call(
        query_kernel,
        out_shape=shape_of((rows, cols)),
        in_specs=[VMEM, VMEM],
        out_specs=VMEM,
        compiler_params=params(8),
        cost_estimate=cost(2 * rows * width * cols, 2 * width * cols),
        name="queries",
    )(latent_in, wq)


def context_kernel(first, step, context_ref, w_ref, after_ref, out_ref):
    def rows_from(i, _):
        there = pl.ds(pl.multiple_of(first + i * step, step), step)
        tile = context_ref[there, :]
        product = dot(tile, w_ref[...]) * inv_rms(tile.astype(F32))
        out_ref[pl.ds(pl.multiple_of(i * step, step), step), :] = product.astype(BF16)
        return 0

    lax.fori_loop(0, out_ref.shape[0] // step, rows_from, 0, unroll=True)


def project_context(context, weight, after, name, first, rows):
    width = context.shape[1]
    cols = weight.shape[1]
    return pl.pallas_call(
        functools.partial(context_kernel, first, min(512, rows)),
        out_shape=shape_of((rows, cols)),
        in_specs=[VMEM, VMEM, pl.BlockSpec(memory_space=pl.ANY)],
        out_specs=VMEM,
        compiler_params=params(20),
        cost_estimate=cost(2 * rows * width * cols, 2 * (rows * width + width * cols)),
        name=name,
    )(context, weight, after)


def packed_totals(totals):
    lane = lax.broadcasted_iota(jnp.int32, totals[0].shape, 1)
    held = jnp.zeros(totals[0].shape, F32)
    for head, total in enumerate(totals):
        held = jnp.where(lane == head, total, held)
    high = held.astype(BF16).astype(F32)
    rest = held - high
    mid = rest.astype(BF16).astype(F32)
    low = rest - mid
    return (high + pltpu.roll(mid, 4, 1) + pltpu.roll(low, 8, 1)).astype(BF16)


def spread_matrix(heads):
    dims = (HEAD_DIM, heads * HEAD_DIM)
    row = lax.broadcasted_iota(jnp.int32, dims, 0)
    head = lax.broadcasted_iota(jnp.int32, dims, 1) >> 7
    return jnp.where((row < 12) & ((row & 3) == head), 1.0, 0.0).astype(BF16)


def cross_kernel(offsets, ids_ref, cutoff_ref, cut_ref, k_ref, more_ref, v_ref, *rest):
    blocks = len(offsets)
    q_refs, out_refs, bias = rest[:blocks], rest[blocks : 2 * blocks], rest[2 * blocks]
    rows, cols = q_refs[0].shape
    heads = cols // HEAD_DIM
    places = v_ref.shape[0]
    step = 512
    first_pos = ids_ref[2]
    starts = [((ids_ref[0] + offset) & 3) * rows for offset in offsets]
    lowest = functools.reduce(jnp.minimum, [cutoff_ref[start] for start in starts])
    highest = functools.reduce(jnp.maximum, [cutoff_ref[start + rows - 1] for start in starts])
    lowest, highest = lowest - first_pos, highest - first_pos
    spans = [slice(head * HEAD_DIM, (head + 1) * HEAD_DIM) for head in range(heads)]

    def stacked(pieces):
        return pieces[0] if blocks == 1 else jnp.concatenate(pieces, axis=0)

    def put(span, value):
        for i, out_ref in enumerate(out_refs):
            out_ref[:, span] = value[i * rows : (i + 1) * rows].astype(BF16)

    @pl.when(highest < 0)
    def _():
        put(slice(0, cols), jnp.zeros((blocks * rows, cols), BF16))
        put(
            slice(cols, cols + HEAD_DIM),
            packed_totals([jnp.full((blocks * rows, HEAD_DIM), MASKED_SCORE, F32)] * heads),
        )

    def attend(masked):
        ones = jnp.ones((step, HEAD_DIM), BF16)
        if masked:
            cut = stacked(
                [cut_ref[pl.ds(pl.multiple_of(start, rows), rows), :] for start in starts]
            )
            cut = cut - first_pos
            order = lax.broadcasted_iota(jnp.int32, cut.shape, 1)
            for place in range(0, places, HEAD_DIM):
                bias[:, place : place + HEAD_DIM] = jnp.where(
                    order + place <= cut, 0.0, MASKED_SCORE
                )

        def scores_of(head):
            queries = stacked([q_ref[:, spans[head]] for q_ref in q_refs])
            keys = jnp.concatenate([k_ref[:, spans[head]], more_ref[:, spans[head]]], axis=0)
            scores = dot_t(queries, keys)
            return scores + bias[...] if masked else scores

        totals = []
        scores = scores_of(0)
        for head in range(heads):
            peak = jnp.max(scores, axis=1, keepdims=True)
            later = scores_of(head + 1) if head + 1 < heads else None
            both = jnp.zeros((blocks * rows, 2 * HEAD_DIM), F32)
            for place in range(0, places, step):
                here = slice(place, place + step)
                probs = jnp.exp2(scores[:, here] - peak).astype(BF16)
                both += dot(probs, jnp.concatenate([v_ref[here, spans[head]], ones], axis=1))
            total = both[:, HEAD_DIM:]
            put(spans[head], both[:, :HEAD_DIM] / total)
            whole = jnp.log2(total) + peak
            totals.append(jnp.where(cut >= 0, whole, MASKED_SCORE) if masked else whole)
            scores = later
        put(slice(cols, cols + HEAD_DIM), packed_totals(totals))

    @pl.when(highest >= 0)
    def _():
        attend(True)


def cross_attend(offsets, ids, cutoff, queries, keys, values, cut_wide):
    blocks = len(offsets)
    rows, cols = queries[0].shape
    places = values.shape[0]
    return pl.pallas_call(
        functools.partial(cross_kernel, offsets),
        out_shape=[shape_of((rows, cols + HEAD_DIM))] * blocks,
        in_specs=[SMEM, SMEM] + [VMEM] * (4 + blocks),
        out_specs=[VMEM] * blocks,
        scratch_shapes=[pltpu.VMEM((blocks * rows, places), F32)],
        compiler_params=params(20 if blocks == 1 else 32),
        cost_estimate=cost(
            blocks * 8 * rows * places * cols, 4 * places * cols, blocks * rows * places * 4
        ),
        name="cross",
    )(ids, cutoff, cut_wide, *keys, values, *queries)


def blend(parts, spread, heads):
    cols = heads * HEAD_DIM
    totals = [dot(part[:, cols:], spread) for part in parts]
    peak = functools.reduce(jnp.maximum, totals)
    weights = [jnp.exp2(total - peak) for total in totals]
    weight_sum = functools.reduce(jnp.add, weights)
    mixed = functools.reduce(
        jnp.add, [w * part[:, :cols].astype(F32) for w, part in zip(weights, parts)]
    )
    return mixed / weight_sum, peak + jnp.log2(weight_sum)


def blend_kernel(a_ref, b_ref, c_ref, d_ref, out_ref):
    rows, width = a_ref.shape
    heads = width // HEAD_DIM - 1
    cols = heads * HEAD_DIM
    mixed, whole = blend(
        [a_ref[...], b_ref[...], c_ref[...], d_ref[...]], spread_matrix(heads), heads
    )
    out_ref[:, :cols] = mixed.astype(BF16)
    out_ref[:, cols:] = packed_totals(
        [whole[:, head * HEAD_DIM : (head + 1) * HEAD_DIM] for head in range(heads)]
    )


def blend_parts(parts):
    return pl.pallas_call(
        blend_kernel,
        out_shape=shape_of(parts[0].shape),
        in_specs=[VMEM] * 4,
        out_specs=VMEM,
        compiler_params=params(16),
        name="blend",
    )(*parts)


def cross_output_kernel(parts_ref, wo_ref, out_ref):
    heads = parts_ref.shape[2] // HEAD_DIM - 1
    parts = [parts_ref[i] for i in range(parts_ref.shape[0])]
    mixed, _ = blend(parts, spread_matrix(heads), heads)
    out_ref[...] = dot(mixed.astype(BF16), wo_ref[...]).astype(BF16)


def cross_output(parts, wo):
    return pl.pallas_call(
        cross_output_kernel,
        out_shape=shape_of((parts.shape[1], wo.shape[1])),
        in_specs=[VMEM] * 2,
        out_specs=VMEM,
        compiler_params=params(16),
        name="cross_output",
    )(parts, wo)


def self_project_kernel(
    ids_ref, latent_ref, one_ref, two_ref, wq_ref, wk_ref, wv_ref, state_ref, *rest
):
    outs, held = rest[:4], rest[4]
    rows, cols = held.shape[1:]
    state = latent_ref[...].astype(F32) + (one_ref[...].astype(F32) + two_ref[...].astype(F32))
    state_ref[...] = state
    normed = (state * inv_rms(state)).astype(BF16)
    held[0] = (dot(normed, wq_ref[...]) * (HEAD_DIM ** (-0.5) * LOG2E)).astype(BF16)
    held[1] = dot(normed, wk_ref[...]).astype(BF16)
    held[2] = dot(normed, wv_ref[...]).astype(BF16)
    for offset in range(4):
        head = lax.rem(ids_ref[0] + offset, 4)
        span = pl.ds(pl.multiple_of(head * HEAD_DIM, HEAD_DIM), HEAD_DIM)
        for part in range(3):
            outs[offset][:, part * HEAD_DIM : (part + 1) * HEAD_DIM] = held[part, :, span]


def self_project(ids, latent_in, one, two, wq, wk, wv):
    rows, width = latent_in.shape
    return pl.pallas_call(
        self_project_kernel,
        out_shape=[shape_of((rows, width), F32)] + [shape_of((rows, 3 * HEAD_DIM))] * 4,
        in_specs=[SMEM] + [VMEM] * 6,
        out_specs=[VMEM] * 5,
        scratch_shapes=[pltpu.VMEM((3, rows, wq.shape[1]), BF16)],
        compiler_params=params(24),
        name="self_project",
    )(ids, latent_in, one, two, wq, wk, wv)


def self_kernel(ids_ref, a_ref, b_ref, c_ref, d_ref, kv_ref, *outs):
    rows = a_ref.shape[0]
    groups, group_rows, _ = kv_ref.shape
    own_a, own_b, stride_a, stride_b, own_y = (ids_ref[i] for i in (0, 1, 3, 4, 5))
    q = jnp.concatenate([ref[:, :HEAD_DIM] for ref in (a_ref, b_ref, c_ref, d_ref)], axis=0)
    k = jnp.concatenate([kv_ref[i, :, :HEAD_DIM] for i in range(groups)], axis=0)
    v = jnp.concatenate([kv_ref[i, :, HEAD_DIM:] for i in range(groups)], axis=0)
    scores = dot_t(q, k)
    q_row = lax.broadcasted_iota(jnp.int32, scores.shape, 0)
    k_row = lax.broadcasted_iota(jnp.int32, scores.shape, 1)
    shift = rows.bit_length() - 1
    q_a = (own_a - (q_row >> shift)) & 3
    q_place = q_a * stride_a + (q_row & (rows - 1)) + (own_b * stride_b + own_y * rows)
    group = k_row >> (group_rows.bit_length() - 1)
    k_a = (own_a - (k_row >> shift)) & 3
    k_place = k_a * stride_a + (group >> 1) * stride_b + (group & 1) * rows + (k_row & (rows - 1))
    scores = jnp.where(k_place <= q_place, scores, MASKED_SCORE)
    peak = jnp.max(scores, axis=1, keepdims=True)
    probs = jnp.exp2(scores - peak).astype(BF16)
    both = dot(probs, jnp.concatenate([v, jnp.ones(v.shape, BF16)], axis=1))
    result = (both[:, :HEAD_DIM] / both[:, HEAD_DIM:]).astype(BF16)
    for offset in range(4):
        outs[offset][...] = result[offset * rows : (offset + 1) * rows]


def self_attend(ids, parts, kv):
    rows = parts[0].shape[0]
    return pl.pallas_call(
        self_kernel,
        out_shape=[shape_of((rows, HEAD_DIM))] * 4,
        in_specs=[SMEM] + [VMEM] * 5,
        out_specs=[VMEM] * 4,
        compiler_params=params(16),
        name="self_attend",
    )(ids, *parts, kv)


def self_output_kernel(ids_ref, a_ref, b_ref, c_ref, d_ref, wo_ref, out_ref, held):
    for offset, ref in enumerate((a_ref, b_ref, c_ref, d_ref)):
        head = lax.rem(ids_ref[0] + offset, 4)
        held[:, pl.ds(pl.multiple_of(head * HEAD_DIM, HEAD_DIM), HEAD_DIM)] = ref[...]
    out_ref[...] = dot(held[...], wo_ref[...]).astype(BF16)


def self_output(ids, parts, wo):
    rows = parts[0].shape[0]
    return pl.pallas_call(
        self_output_kernel,
        out_shape=shape_of((rows, wo.shape[1])),
        in_specs=[SMEM] + [VMEM] * 5,
        out_specs=VMEM,
        scratch_shapes=[pltpu.VMEM((rows, wo.shape[0]), BF16)],
        compiler_params=params(16),
        name="self_output",
    )(ids, *parts, wo)


def moved(tensor, axis, size, offset):
    return lax.ppermute(tensor, axis, [(i, (i + offset) % size) for i in range(size)])


PLANE = ("x", "z", "core")
WHOLE = ("x", "z", "y_lo", "y_hi", "core")


def turned(tensor, axis, offset):
    pairs = []
    for x in range(4):
        for z in range(4):
            for core in range(2):
                if (axis == "a") == (core == 0):
                    to = ((x + offset) % 4, z)
                else:
                    to = (x, (z + offset) % 4)
                pairs.append(((x * 4 + z) * 2 + core, (to[0] * 4 + to[1]) * 2 + core))
    return lax.ppermute(tensor, PLANE, pairs)


def exchanged(tensor):
    order = np.arange(128).reshape(4, 4, 2, 2, 2)
    groups = []
    for y_hi in range(2):
        for a in range(4):
            groups.append(order[a, :, :, y_hi, 0].reshape(-1).tolist())
            groups.append(order[:, a, :, y_hi, 1].reshape(-1).tolist())
    return lax.all_to_all(tensor, WHOLE, 0, 0, axis_index_groups=groups)


def summed_over_tp(part):
    other = moved(part, "core", 2, 1)
    pair = (part.astype(F32) + other.astype(F32)).astype(BF16)
    return pair, moved(pair, "y_hi", 2, 1)


def on_device(
    context,
    latent_in,
    cutoff,
    wq_cross,
    wk_cross,
    wv_cross,
    wo_cross,
    wq_self,
    wk_self,
    wv_self,
    wo_self,
):
    x, z, y_lo = lax.axis_index("x"), lax.axis_index("z"), lax.axis_index("y_lo")
    first_core = lax.axis_index("core") == 0
    a = jnp.where(first_core, x, z)
    b = jnp.where(first_core, z, x)
    rows = latent_in.shape[0]
    stride_a = jnp.where(first_core, 8 * rows, 2 * rows)
    stride_b = jnp.where(first_core, 2 * rows, 8 * rows)
    first_pos = ((x * 4 + z) * 2 + y_lo) * context.shape[0]
    ids = jnp.stack([a, b, first_pos, stride_a, stride_b, y_lo]).astype(jnp.int32)
    turned_cutoff = cutoff.reshape(4, 4, 2 * rows).transpose(1, 0, 2).reshape(-1)
    cutoff = jnp.where(first_core, cutoff, turned_cutoff)
    cut_wide = jnp.broadcast_to(cutoff[:, None], (cutoff.shape[0], HEAD_DIM))

    own = project_queries(latent_in, wq_cross)
    other = moved(own, "y_lo", 2, 1)
    pair = jnp.where(
        y_lo == 0, jnp.concatenate([own, other]), jnp.concatenate([other, own])
    )
    half = context.shape[0] // 2
    keys = [project_context(context, wk_cross, pair, "keys", 0, half)]
    came = {offset: turned(pair, "b", offset) for offset in (2, 1, 3)}
    ring = [pair] + [came[offset] for offset in (1, 2, 3)]
    pieces = [
        lax.dynamic_index_in_dim(jnp.stack(ring), (b - place) & 3, 0, False) for place in range(4)
    ]
    mine = jnp.concatenate(pieces)
    keys.append(project_context(context, wk_cross, mine, "keys", half, half))
    values = project_context(context, wv_cross, mine, "values", 0, 2 * half)
    blocks = {0: mine}
    for offset in (2, 3, 1):
        blocks[(4 - offset) % 4] = turned(mine, "a", offset)

    parts = []
    for offsets in ((2, 1), (3,), (0,)):
        queries = [blocks[offset] for offset in offsets]
        made = cross_attend(offsets, ids, cutoff, queries, keys, values, cut_wide)
        for offset, part in zip(offsets, made):
            parts.append(turned(part, "a", offset) if offset else part)
    mixed = blend_parts(parts)
    mixed = mixed.reshape(8, rows, mixed.shape[1])
    mixed = exchanged(mixed)
    cross_part = cross_output(mixed, wo_cross)
    one, two = summed_over_tp(cross_part)

    state, *sent = self_project(ids, latent_in, one, two, wq_self, wk_self, wv_self)
    came = {o: turned(sent[o], "a", o) for o in (2, 1, 3)}
    parts = [sent[0]] + [came[o] for o in (1, 2, 3)]
    kv = jnp.concatenate([part[:, HEAD_DIM:] for part in parts])
    kv = exchanged(jnp.broadcast_to(kv[None], (8,) + kv.shape))
    outs = self_attend(ids, parts, kv)
    came = {o: turned(outs[o], "a", -o) for o in (2, 1, 3)}
    outs = [outs[0]] + [came[o] for o in (1, 2, 3)]
    self_part = self_output(ids, outs, wo_self)
    one, two = summed_over_tp(self_part)
    return (state + (one.astype(F32) + two.astype(F32))).astype(BF16)


def solution(mesh):
    fine = Mesh(
        mesh.devices.reshape(4, 4, 2, 2, 2), ("x", "z", "y_lo", "y_hi", "core")
    )
    seq, tp = ("x", "z", "y_lo"), ("y_hi", "core")
    in_specs = (
        P(seq, None),
        P(seq, None),
        P(),
        P(None, tp),
        P(None, tp),
        P(None, tp),
        P(tp, None),
        P(None, tp),
        P(None, tp),
        P(None, tp),
        P(tp, None),
    )
    return jax.shard_map(
        on_device, mesh=fine, in_specs=in_specs, out_specs=P(seq, None), check_vma=False
    )
```

```python
import functools

import jax
import jax.numpy as jnp
import numpy as np
from jax import lax
from jax.experimental import pallas as pl
from jax.experimental.pallas import tpu as pltpu
from jax.sharding import Mesh, PartitionSpec as P

HEAD_DIM = 128
EPSILON = 1e-05
MASKED_SCORE = -1e30
LOG2E = 1.4426950408889634
MIB = 1 << 20
F32 = jnp.float32
BF16 = jnp.bfloat16

VMEM = pl.BlockSpec(memory_space=pltpu.VMEM)
HBM = pl.BlockSpec(memory_space=pltpu.HBM)
SMEM = pl.BlockSpec(memory_space=pltpu.SMEM)


def shape_of(dims, dtype=BF16):
    return jax.ShapeDtypeStruct(dims, dtype)


def params(mib):
    return pltpu.CompilerParams(vmem_limit_bytes=mib * MIB)


def cost(flops, nbytes, trans=0):
    return pl.CostEstimate(flops=flops, bytes_accessed=nbytes, transcendentals=trans)


def dot(a, b):
    return jnp.dot(a, b, preferred_element_type=F32)


def dot_t(a, b):
    return lax.dot_general(a, b, (((1,), (1,)), ((), ())), preferred_element_type=F32)


def inv_rms(tile):
    return lax.rsqrt(jnp.mean(tile * tile, axis=-1, keepdims=True) + EPSILON)


def query_kernel(latent_ref, wq_ref, out_ref, latent, weight, sems):
    pieces = weight.shape[0]
    depth = weight.shape[1]
    first = pltpu.make_async_copy(latent_ref, latent, sems.at[pieces])
    copies = [
        pltpu.make_async_copy(wq_ref.at[pl.ds(i * depth, depth)], weight.at[i], sems.at[i])
        for i in range(pieces)
    ]
    for copy in [first] + copies:
        copy.start()
    first.wait()
    tile = latent[...].astype(F32)
    normed = (tile * inv_rms(tile)).astype(BF16)
    total = jnp.zeros(out_ref.shape, F32)
    for i, copy in enumerate(copies):
        copy.wait()
        total += dot(normed[:, i * depth : (i + 1) * depth], weight[i])
    out_ref[...] = (total * (HEAD_DIM ** (-0.5) * LOG2E)).astype(BF16)


def project_queries(latent_in, wq):
    rows, width = latent_in.shape
    cols = wq.shape[1]
    pieces = 4
    return pl.pallas_call(
        query_kernel,
        out_shape=shape_of((rows, cols)),
        in_specs=[HBM, HBM],
        out_specs=VMEM,
        scratch_shapes=[
            pltpu.VMEM((rows, width), BF16),
            pltpu.VMEM((pieces, width // pieces, cols), BF16),
            pltpu.SemaphoreType.DMA((pieces + 1,)),
        ],
        compiler_params=params(20),
        cost_estimate=cost(2 * rows * width * cols, 2 * width * cols),
        name="queries",
    )(
        pltpu.with_memory_space_constraint(latent_in, pltpu.HBM),
        pltpu.with_memory_space_constraint(wq, pltpu.HBM),
    )


def context_kernel(first, step, context_ref, w_ref, after_ref, out_ref):
    def rows_from(i, _):
        there = pl.ds(pl.multiple_of(first + i * step, step), step)
        tile = context_ref[there, :]
        product = dot(tile, w_ref[...]) * inv_rms(tile.astype(F32))
        out_ref[pl.ds(pl.multiple_of(i * step, step), step), :] = product.astype(BF16)
        return 0

    lax.fori_loop(0, out_ref.shape[0] // step, rows_from, 0, unroll=True)


def project_context(context, weight, after, name, first, rows):
    width = context.shape[1]
    cols = weight.shape[1]
    return pl.pallas_call(
        functools.partial(context_kernel, first, min(512, rows)),
        out_shape=shape_of((rows, cols)),
        in_specs=[VMEM, VMEM, pl.BlockSpec(memory_space=pl.ANY)],
        out_specs=VMEM,
        compiler_params=params(20),
        cost_estimate=cost(2 * rows * width * cols, 2 * (rows * width + width * cols)),
        name=name,
    )(context, weight, after)


def packed_totals(totals):
    lane = lax.broadcasted_iota(jnp.int32, totals[0].shape, 1)
    held = jnp.zeros(totals[0].shape, F32)
    for head, total in enumerate(totals):
        held = jnp.where(lane == head, total, held)
    high = held.astype(BF16).astype(F32)
    rest = held - high
    mid = rest.astype(BF16).astype(F32)
    low = rest - mid
    return (high + pltpu.roll(mid, 4, 1) + pltpu.roll(low, 8, 1)).astype(BF16)


def spread_matrix(heads):
    dims = (HEAD_DIM, heads * HEAD_DIM)
    row = lax.broadcasted_iota(jnp.int32, dims, 0)
    head = lax.broadcasted_iota(jnp.int32, dims, 1) >> 7
    return jnp.where((row < 12) & ((row & 3) == head), 1.0, 0.0).astype(BF16)


def cross_kernel(offsets, ids_ref, cutoff_ref, cut_ref, k_ref, more_ref, v_ref, *rest):
    blocks = len(offsets)
    q_refs, out_refs, bias = rest[:blocks], rest[blocks : 2 * blocks], rest[2 * blocks]
    rows, cols = q_refs[0].shape
    heads = cols // HEAD_DIM
    places = v_ref.shape[0]
    step = 512
    first_pos = ids_ref[2]
    starts = [((ids_ref[0] + offset) & 3) * rows for offset in offsets]
    lowest = functools.reduce(jnp.minimum, [cutoff_ref[start] for start in starts])
    highest = functools.reduce(jnp.maximum, [cutoff_ref[start + rows - 1] for start in starts])
    lowest, highest = lowest - first_pos, highest - first_pos
    spans = [slice(head * HEAD_DIM, (head + 1) * HEAD_DIM) for head in range(heads)]

    def stacked(pieces):
        return pieces[0] if blocks == 1 else jnp.concatenate(pieces, axis=0)

    def put(span, value):
        for i, out_ref in enumerate(out_refs):
            out_ref[:, span] = value[i * rows : (i + 1) * rows].astype(BF16)

    @pl.when(highest < 0)
    def _():
        put(slice(0, cols), jnp.zeros((blocks * rows, cols), BF16))
        put(
            slice(cols, cols + HEAD_DIM),
            packed_totals([jnp.full((blocks * rows, HEAD_DIM), MASKED_SCORE, F32)] * heads),
        )

    def attend(masked):
        ones = jnp.ones((step, HEAD_DIM), BF16)
        if masked:
            cut = stacked(
                [cut_ref[pl.ds(pl.multiple_of(start, rows), rows), :] for start in starts]
            )
            cut = cut - first_pos
            order = lax.broadcasted_iota(jnp.int32, cut.shape, 1)
            for place in range(0, places, HEAD_DIM):
                bias[:, place : place + HEAD_DIM] = jnp.where(
                    order + place <= cut, 0.0, MASKED_SCORE
                )

        def scores_of(head):
            queries = stacked([q_ref[:, spans[head]] for q_ref in q_refs])
            keys = jnp.concatenate([k_ref[:, spans[head]], more_ref[:, spans[head]]], axis=0)
            scores = dot_t(queries, keys)
            return scores + bias[...] if masked else scores

        totals = []
        scores = scores_of(0)
        for head in range(heads):
            peak = jnp.max(scores, axis=1, keepdims=True)
            later = scores_of(head + 1) if head + 1 < heads else None
            both = jnp.zeros((blocks * rows, 2 * HEAD_DIM), F32)
            for place in range(0, places, step):
                here = slice(place, place + step)
                probs = jnp.exp2(scores[:, here] - peak).astype(BF16)
                both += dot(probs, jnp.concatenate([v_ref[here, spans[head]], ones], axis=1))
            total = both[:, HEAD_DIM:]
            put(spans[head], both[:, :HEAD_DIM] / total)
            whole = jnp.log2(total) + peak
            totals.append(jnp.where(cut >= 0, whole, MASKED_SCORE) if masked else whole)
            scores = later
        put(slice(cols, cols + HEAD_DIM), packed_totals(totals))

    @pl.when(highest >= 0)
    def _():
        attend(True)


def cross_attend(offsets, ids, cutoff, queries, keys, values, cut_wide):
    blocks = len(offsets)
    rows, cols = queries[0].shape
    places = values.shape[0]
    return pl.pallas_call(
        functools.partial(cross_kernel, offsets),
        out_shape=[shape_of((rows, cols + HEAD_DIM))] * blocks,
        in_specs=[SMEM, SMEM] + [VMEM] * (4 + blocks),
        out_specs=[VMEM] * blocks,
        scratch_shapes=[pltpu.VMEM((blocks * rows, places), F32)],
        compiler_params=params(20 if blocks == 1 else 32),
        cost_estimate=cost(
            blocks * 8 * rows * places * cols, 4 * places * cols, blocks * rows * places * 4
        ),
        name="cross",
    )(ids, cutoff, cut_wide, *keys, values, *queries)


def blend(parts, spread, heads):
    cols = heads * HEAD_DIM
    totals = [dot(part[:, cols:], spread) for part in parts]
    peak = functools.reduce(jnp.maximum, totals)
    weights = [jnp.exp2(total - peak) for total in totals]
    weight_sum = functools.reduce(jnp.add, weights)
    mixed = functools.reduce(
        jnp.add, [w * part[:, :cols].astype(F32) for w, part in zip(weights, parts)]
    )
    return mixed / weight_sum, peak + jnp.log2(weight_sum)


def blend_kernel(a_ref, b_ref, c_ref, d_ref, out_ref):
    rows, width = a_ref.shape
    heads = width // HEAD_DIM - 1
    cols = heads * HEAD_DIM
    mixed, whole = blend(
        [a_ref[...], b_ref[...], c_ref[...], d_ref[...]], spread_matrix(heads), heads
    )
    out_ref[:, :cols] = mixed.astype(BF16)
    out_ref[:, cols:] = packed_totals(
        [whole[:, head * HEAD_DIM : (head + 1) * HEAD_DIM] for head in range(heads)]
    )


def blend_parts(parts):
    return pl.pallas_call(
        blend_kernel,
        out_shape=shape_of(parts[0].shape),
        in_specs=[VMEM] * 4,
        out_specs=VMEM,
        compiler_params=params(16),
        name="blend",
    )(*parts)


def cross_output_kernel(parts_ref, wo_ref, out_ref):
    heads = parts_ref.shape[2] // HEAD_DIM - 1
    parts = [parts_ref[i] for i in range(parts_ref.shape[0])]
    mixed, _ = blend(parts, spread_matrix(heads), heads)
    out_ref[...] = dot(mixed.astype(BF16), wo_ref[...]).astype(BF16)


def cross_output(parts, wo):
    return pl.pallas_call(
        cross_output_kernel,
        out_shape=shape_of((parts.shape[1], wo.shape[1])),
        in_specs=[VMEM] * 2,
        out_specs=VMEM,
        compiler_params=params(16),
        name="cross_output",
    )(parts, wo)


def self_project_kernel(
    ids_ref, latent_ref, one_ref, two_ref, wq_ref, wk_ref, wv_ref, state_ref, *rest
):
    outs, held = rest[:4], rest[4]
    rows, cols = held.shape[1:]
    state = latent_ref[...].astype(F32) + (one_ref[...].astype(F32) + two_ref[...].astype(F32))
    state_ref[...] = state
    normed = (state * inv_rms(state)).astype(BF16)
    held[0] = (dot(normed, wq_ref[...]) * (HEAD_DIM ** (-0.5) * LOG2E)).astype(BF16)
    held[1] = dot(normed, wk_ref[...]).astype(BF16)
    held[2] = dot(normed, wv_ref[...]).astype(BF16)
    for offset in range(4):
        head = lax.rem(ids_ref[0] + offset, 4)
        span = pl.ds(pl.multiple_of(head * HEAD_DIM, HEAD_DIM), HEAD_DIM)
        for part in range(3):
            outs[offset][:, part * HEAD_DIM : (part + 1) * HEAD_DIM] = held[part, :, span]


def self_project(ids, latent_in, one, two, wq, wk, wv):
    rows, width = latent_in.shape
    return pl.pallas_call(
        self_project_kernel,
        out_shape=[shape_of((rows, width), F32)] + [shape_of((rows, 3 * HEAD_DIM))] * 4,
        in_specs=[SMEM] + [VMEM] * 6,
        out_specs=[VMEM] * 5,
        scratch_shapes=[pltpu.VMEM((3, rows, wq.shape[1]), BF16)],
        compiler_params=params(24),
        name="self_project",
    )(ids, latent_in, one, two, wq, wk, wv)


def self_kernel(ids_ref, a_ref, b_ref, c_ref, d_ref, kv_ref, *outs):
    rows = a_ref.shape[0]
    groups, group_rows, _ = kv_ref.shape
    own_a, own_b, stride_a, stride_b, own_y = (ids_ref[i] for i in (0, 1, 3, 4, 5))
    q = jnp.concatenate([ref[:, :HEAD_DIM] for ref in (a_ref, b_ref, c_ref, d_ref)], axis=0)
    k = jnp.concatenate([kv_ref[i, :, :HEAD_DIM] for i in range(groups)], axis=0)
    v = jnp.concatenate([kv_ref[i, :, HEAD_DIM:] for i in range(groups)], axis=0)
    scores = dot_t(q, k)
    q_row = lax.broadcasted_iota(jnp.int32, scores.shape, 0)
    k_row = lax.broadcasted_iota(jnp.int32, scores.shape, 1)
    shift = rows.bit_length() - 1
    q_a = (own_a - (q_row >> shift)) & 3
    q_place = q_a * stride_a + (q_row & (rows - 1)) + (own_b * stride_b + own_y * rows)
    group = k_row >> (group_rows.bit_length() - 1)
    k_a = (own_a - (k_row >> shift)) & 3
    k_place = k_a * stride_a + (group >> 1) * stride_b + (group & 1) * rows + (k_row & (rows - 1))
    scores = jnp.where(k_place <= q_place, scores, MASKED_SCORE)
    peak = jnp.max(scores, axis=1, keepdims=True)
    probs = jnp.exp2(scores - peak).astype(BF16)
    both = dot(probs, jnp.concatenate([v, jnp.ones(v.shape, BF16)], axis=1))
    result = (both[:, :HEAD_DIM] / both[:, HEAD_DIM:]).astype(BF16)
    for offset in range(4):
        outs[offset][...] = result[offset * rows : (offset + 1) * rows]


def self_attend(ids, parts, kv):
    rows = parts[0].shape[0]
    return pl.pallas_call(
        self_kernel,
        out_shape=[shape_of((rows, HEAD_DIM))] * 4,
        in_specs=[SMEM] + [VMEM] * 5,
        out_specs=[VMEM] * 4,
        compiler_params=params(16),
        name="self_attend",
    )(ids, *parts, kv)


def self_output_kernel(ids_ref, a_ref, b_ref, c_ref, d_ref, wo_ref, out_ref, held):
    for offset, ref in enumerate((a_ref, b_ref, c_ref, d_ref)):
        head = lax.rem(ids_ref[0] + offset, 4)
        held[:, pl.ds(pl.multiple_of(head * HEAD_DIM, HEAD_DIM), HEAD_DIM)] = ref[...]
    out_ref[...] = dot(held[...], wo_ref[...]).astype(BF16)


def self_output(ids, parts, wo):
    rows = parts[0].shape[0]
    return pl.pallas_call(
        self_output_kernel,
        out_shape=shape_of((rows, wo.shape[1])),
        in_specs=[SMEM] + [VMEM] * 5,
        out_specs=VMEM,
        scratch_shapes=[pltpu.VMEM((rows, wo.shape[0]), BF16)],
        compiler_params=params(16),
        name="self_output",
    )(ids, *parts, wo)


def moved(tensor, axis, size, offset):
    return lax.ppermute(tensor, axis, [(i, (i + offset) % size) for i in range(size)])


PLANE = ("x", "z", "core")
WHOLE = ("x", "z", "y_lo", "y_hi", "core")


def turned(tensor, axis, offset):
    pairs = []
    for x in range(4):
        for z in range(4):
            for core in range(2):
                if (axis == "a") == (core == 0):
                    to = ((x + offset) % 4, z)
                else:
                    to = (x, (z + offset) % 4)
                pairs.append(((x * 4 + z) * 2 + core, (to[0] * 4 + to[1]) * 2 + core))
    return lax.ppermute(tensor, PLANE, pairs)


def exchanged(tensor):
    order = np.arange(128).reshape(4, 4, 2, 2, 2)
    groups = []
    for y_hi in range(2):
        for a in range(4):
            groups.append(order[a, :, :, y_hi, 0].reshape(-1).tolist())
            groups.append(order[:, a, :, y_hi, 1].reshape(-1).tolist())
    return lax.all_to_all(tensor, WHOLE, 0, 0, axis_index_groups=groups)


def summed_over_tp(part):
    other = moved(part, "core", 2, 1)
    pair = (part.astype(F32) + other.astype(F32)).astype(BF16)
    return pair, moved(pair, "y_hi", 2, 1)


def on_device(
    context,
    latent_in,
    cutoff,
    wq_cross,
    wk_cross,
    wv_cross,
    wo_cross,
    wq_self,
    wk_self,
    wv_self,
    wo_self,
):
    x, z, y_lo = lax.axis_index("x"), lax.axis_index("z"), lax.axis_index("y_lo")
    first_core = lax.axis_index("core") == 0
    a = jnp.where(first_core, x, z)
    b = jnp.where(first_core, z, x)
    rows = latent_in.shape[0]
    stride_a = jnp.where(first_core, 8 * rows, 2 * rows)
    stride_b = jnp.where(first_core, 2 * rows, 8 * rows)
    first_pos = ((x * 4 + z) * 2 + y_lo) * context.shape[0]
    ids = jnp.stack([a, b, first_pos, stride_a, stride_b, y_lo]).astype(jnp.int32)
    turned_cutoff = cutoff.reshape(4, 4, 2 * rows).transpose(1, 0, 2).reshape(-1)
    cutoff = jnp.where(first_core, cutoff, turned_cutoff)
    cut_wide = jnp.broadcast_to(cutoff[:, None], (cutoff.shape[0], HEAD_DIM))

    own = project_queries(latent_in, wq_cross)
    other = moved(own, "y_lo", 2, 1)
    pair = jnp.where(
        y_lo == 0, jnp.concatenate([own, other]), jnp.concatenate([other, own])
    )
    half = context.shape[0] // 2
    keys = [project_context(context, wk_cross, pair, "keys", 0, half)]
    came = {offset: turned(pair, "b", offset) for offset in (2, 1, 3)}
    ring = [pair] + [came[offset] for offset in (1, 2, 3)]
    pieces = [
        lax.dynamic_index_in_dim(jnp.stack(ring), (b - place) & 3, 0, False) for place in range(4)
    ]
    mine = jnp.concatenate(pieces)
    keys.append(project_context(context, wk_cross, mine, "keys", half, half))
    values = project_context(context, wv_cross, mine, "values", 0, 2 * half)
    blocks = {0: mine}
    for offset in (2, 3, 1):
        blocks[(4 - offset) % 4] = turned(mine, "a", offset)

    parts = []
    for offsets in ((2, 1), (3,), (0,)):
        queries = [blocks[offset] for offset in offsets]
        made = cross_attend(offsets, ids, cutoff, queries, keys, values, cut_wide)
        for offset, part in zip(offsets, made):
            parts.append(turned(part, "a", offset) if offset else part)
    mixed = blend_parts(parts)
    mixed = mixed.reshape(8, rows, mixed.shape[1])
    mixed = exchanged(mixed)
    cross_part = cross_output(mixed, wo_cross)
    one, two = summed_over_tp(cross_part)

    state, *sent = self_project(ids, latent_in, one, two, wq_self, wk_self, wv_self)
    came = {o: turned(sent[o], "a", o) for o in (2, 1, 3)}
    parts = [sent[0]] + [came[o] for o in (1, 2, 3)]
    kv = jnp.concatenate([part[:, HEAD_DIM:] for part in parts])
    kv = exchanged(jnp.broadcast_to(kv[None], (8,) + kv.shape))
    outs = self_attend(ids, parts, kv)
    came = {o: turned(outs[o], "a", -o) for o in (2, 1, 3)}
    outs = [outs[0]] + [came[o] for o in (1, 2, 3)]
    self_part = self_output(ids, outs, wo_self)
    one, two = summed_over_tp(self_part)
    return (state + (one.astype(F32) + two.astype(F32))).astype(BF16)


def solution(mesh):
    fine = Mesh(
        mesh.devices.reshape(4, 4, 2, 2, 2), ("x", "z", "y_lo", "y_hi", "core")
    )
    seq, tp = ("x", "z", "y_lo"), ("y_hi", "core")
    in_specs = (
        P(seq, None),
        P(seq, None),
        P(),
        P(None, tp),
        P(None, tp),
        P(None, tp),
        P(tp, None),
        P(None, tp),
        P(None, tp),
        P(None, tp),
        P(tp, None),
    )
    return jax.shard_map(
        on_device, mesh=fine, in_specs=in_specs, out_specs=P(seq, None), check_vma=False
    )
```

```python
import functools

import jax
import jax.numpy as jnp
import numpy as np
from jax import lax
from jax.experimental import pallas as pl
from jax.experimental.pallas import tpu as pltpu
from jax.sharding import Mesh, PartitionSpec as P

HEAD_DIM = 128
EPSILON = 1e-05
MASKED_SCORE = -1e30
LOG2E = 1.4426950408889634
MIB = 1 << 20
F32 = jnp.float32
BF16 = jnp.bfloat16

VMEM = pl.BlockSpec(memory_space=pltpu.VMEM)
HBM = pl.BlockSpec(memory_space=pltpu.HBM)
SMEM = pl.BlockSpec(memory_space=pltpu.SMEM)


def shape_of(dims, dtype=BF16):
    return jax.ShapeDtypeStruct(dims, dtype)


def params(mib):
    return pltpu.CompilerParams(vmem_limit_bytes=mib * MIB)


def cost(flops, nbytes, trans=0):
    return pl.CostEstimate(flops=flops, bytes_accessed=nbytes, transcendentals=trans)


def dot(a, b):
    return jnp.dot(a, b, preferred_element_type=F32)


def dot_t(a, b):
    return lax.dot_general(a, b, (((1,), (1,)), ((), ())), preferred_element_type=F32)


def inv_rms(tile):
    return lax.rsqrt(jnp.mean(tile * tile, axis=-1, keepdims=True) + EPSILON)


def query_kernel(latent_ref, wq_ref, out_ref, latent, weight, sems):
    pieces = weight.shape[0]
    depth = weight.shape[1]
    first = pltpu.make_async_copy(latent_ref, latent, sems.at[pieces])
    copies = [
        pltpu.make_async_copy(wq_ref.at[pl.ds(i * depth, depth)], weight.at[i], sems.at[i])
        for i in range(pieces)
    ]
    for copy in [first] + copies:
        copy.start()
    first.wait()
    tile = latent[...].astype(F32)
    normed = (tile * inv_rms(tile)).astype(BF16)
    total = jnp.zeros(out_ref.shape, F32)
    for i, copy in enumerate(copies):
        copy.wait()
        total += dot(normed[:, i * depth : (i + 1) * depth], weight[i])
    out_ref[...] = (total * (HEAD_DIM ** (-0.5) * LOG2E)).astype(BF16)


def project_queries(latent_in, wq):
    rows, width = latent_in.shape
    cols = wq.shape[1]
    pieces = 4
    return pl.pallas_call(
        query_kernel,
        out_shape=shape_of((rows, cols)),
        in_specs=[HBM, HBM],
        out_specs=VMEM,
        scratch_shapes=[
            pltpu.VMEM((rows, width), BF16),
            pltpu.VMEM((pieces, width // pieces, cols), BF16),
            pltpu.SemaphoreType.DMA((pieces + 1,)),
        ],
        compiler_params=params(20),
        cost_estimate=cost(2 * rows * width * cols, 2 * width * cols),
        name="queries",
    )(
        pltpu.with_memory_space_constraint(latent_in, pltpu.HBM),
        pltpu.with_memory_space_constraint(wq, pltpu.HBM),
    )


def context_kernel(first, step, context_ref, w_ref, after_ref, out_ref):
    def rows_from(i, _):
        there = pl.ds(pl.multiple_of(first + i * step, step), step)
        tile = context_ref[there, :]
        product = dot(tile, w_ref[...]) * inv_rms(tile.astype(F32))
        out_ref[pl.ds(pl.multiple_of(i * step, step), step), :] = product.astype(BF16)
        return 0

    lax.fori_loop(0, out_ref.shape[0] // step, rows_from, 0, unroll=True)


def project_context(context, weight, after, name, first, rows):
    width = context.shape[1]
    cols = weight.shape[1]
    return pl.pallas_call(
        functools.partial(context_kernel, first, 512 if rows % 512 == 0 else 256),
        out_shape=shape_of((rows, cols)),
        in_specs=[VMEM, VMEM, pl.BlockSpec(memory_space=pl.ANY)],
        out_specs=VMEM,
        compiler_params=params(20),
        cost_estimate=cost(2 * rows * width * cols, 2 * (rows * width + width * cols)),
        name=name,
    )(context, weight, after)


def first_kernel(context_ref, w_ref, after_ref, out_ref, held, sems):
    pieces, step = held.shape[:2]
    copies = [
        pltpu.make_async_copy(context_ref.at[pl.ds(i * step, step)], held.at[i], sems.at[i])
        for i in range(pieces)
    ]
    for copy in copies:
        copy.start()
    for i, copy in enumerate(copies):
        copy.wait()
        tile = held[i]
        product = dot(tile, w_ref[...]) * inv_rms(tile.astype(F32))
        out_ref[pl.ds(i * step, step), :] = product.astype(BF16)


def first_project(context, weight, after, rows):
    width = context.shape[1]
    cols = weight.shape[1]
    pieces = 4
    return pl.pallas_call(
        first_kernel,
        out_shape=shape_of((rows, cols)),
        in_specs=[HBM, VMEM, pl.BlockSpec(memory_space=pl.ANY)],
        out_specs=VMEM,
        scratch_shapes=[
            pltpu.VMEM((pieces, rows // pieces, width), BF16),
            pltpu.SemaphoreType.DMA((pieces,)),
        ],
        compiler_params=params(20),
        cost_estimate=cost(2 * rows * width * cols, 2 * (rows * width + width * cols)),
        name="first_keys",
    )(pltpu.with_memory_space_constraint(context, pltpu.HBM), weight, after)


def packed_totals(totals):
    lane = lax.broadcasted_iota(jnp.int32, totals[0].shape, 1)
    held = jnp.zeros(totals[0].shape, F32)
    for head, total in enumerate(totals):
        held = jnp.where(lane == head, total, held)
    high = held.astype(BF16).astype(F32)
    rest = held - high
    mid = rest.astype(BF16).astype(F32)
    low = rest - mid
    return (high + pltpu.roll(mid, 4, 1) + pltpu.roll(low, 8, 1)).astype(BF16)


def spread_matrix(heads):
    dims = (HEAD_DIM, heads * HEAD_DIM)
    row = lax.broadcasted_iota(jnp.int32, dims, 0)
    head = lax.broadcasted_iota(jnp.int32, dims, 1) >> 7
    return jnp.where((row < 12) & ((row & 3) == head), 1.0, 0.0).astype(BF16)


def cross_kernel(offsets, ids_ref, cutoff_ref, cut_ref, k_ref, more_ref, v_ref, *rest):
    blocks = len(offsets)
    q_refs, out_refs, bias = rest[:blocks], rest[blocks : 2 * blocks], rest[2 * blocks]
    rows, cols = q_refs[0].shape
    heads = cols // HEAD_DIM
    places = v_ref.shape[0]
    step = 512
    first_pos = ids_ref[2]
    starts = [((ids_ref[0] + offset) & 3) * rows for offset in offsets]
    lowest = functools.reduce(jnp.minimum, [cutoff_ref[start] for start in starts])
    highest = functools.reduce(jnp.maximum, [cutoff_ref[start + rows - 1] for start in starts])
    lowest, highest = lowest - first_pos, highest - first_pos
    spans = [slice(head * HEAD_DIM, (head + 1) * HEAD_DIM) for head in range(heads)]

    def stacked(pieces):
        return pieces[0] if blocks == 1 else jnp.concatenate(pieces, axis=0)

    def put(span, value):
        for i, out_ref in enumerate(out_refs):
            out_ref[:, span] = value[i * rows : (i + 1) * rows].astype(BF16)

    @pl.when(highest < 0)
    def _():
        put(slice(0, cols), jnp.zeros((blocks * rows, cols), BF16))
        put(
            slice(cols, cols + HEAD_DIM),
            packed_totals([jnp.full((blocks * rows, HEAD_DIM), MASKED_SCORE, F32)] * heads),
        )

    def attend(masked):
        ones = jnp.ones((step, HEAD_DIM), BF16)
        if masked:
            cut = stacked(
                [cut_ref[pl.ds(pl.multiple_of(start, rows), rows), :] for start in starts]
            )
            cut = cut - first_pos
            order = lax.broadcasted_iota(jnp.int32, cut.shape, 1)
            for place in range(0, places, HEAD_DIM):
                bias[:, place : place + HEAD_DIM] = jnp.where(
                    order + place <= cut, 0.0, MASKED_SCORE
                )

        def scores_of(head):
            queries = stacked([q_ref[:, spans[head]] for q_ref in q_refs])
            keys = jnp.concatenate([k_ref[:, spans[head]], more_ref[:, spans[head]]], axis=0)
            scores = dot_t(queries, keys)
            return scores + bias[...] if masked else scores

        totals = []
        scores = scores_of(0)
        for head in range(heads):
            peak = jnp.max(scores, axis=1, keepdims=True)
            later = scores_of(head + 1) if head + 1 < heads else None
            both = jnp.zeros((blocks * rows, 2 * HEAD_DIM), F32)
            for place in range(0, places, step):
                here = slice(place, place + step)
                probs = jnp.exp2(scores[:, here] - peak).astype(BF16)
                both += dot(probs, jnp.concatenate([v_ref[here, spans[head]], ones], axis=1))
            total = both[:, HEAD_DIM:]
            put(spans[head], both[:, :HEAD_DIM] / total)
            whole = jnp.log2(total) + peak
            totals.append(jnp.where(cut >= 0, whole, MASKED_SCORE) if masked else whole)
            scores = later
        put(slice(cols, cols + HEAD_DIM), packed_totals(totals))

    @pl.when(highest >= 0)
    def _():
        attend(True)


def cross_attend(offsets, ids, cutoff, queries, keys, values, cut_wide):
    blocks = len(offsets)
    rows, cols = queries[0].shape
    places = values.shape[0]
    return pl.pallas_call(
        functools.partial(cross_kernel, offsets),
        out_shape=[shape_of((rows, cols + HEAD_DIM))] * blocks,
        in_specs=[SMEM, SMEM] + [VMEM] * (4 + blocks),
        out_specs=[VMEM] * blocks,
        scratch_shapes=[pltpu.VMEM((blocks * rows, places), F32)],
        compiler_params=params(20 if blocks == 1 else 32),
        cost_estimate=cost(
            blocks * 8 * rows * places * cols, 4 * places * cols, blocks * rows * places * 4
        ),
        name="cross",
    )(ids, cutoff, cut_wide, *keys, values, *queries)


def blend(parts, spread, heads):
    cols = heads * HEAD_DIM
    totals = [dot(part[:, cols:], spread) for part in parts]
    peak = functools.reduce(jnp.maximum, totals)
    weights = [jnp.exp2(total - peak) for total in totals]
    weight_sum = functools.reduce(jnp.add, weights)
    mixed = functools.reduce(
        jnp.add, [w * part[:, :cols].astype(F32) for w, part in zip(weights, parts)]
    )
    return mixed / weight_sum, peak + jnp.log2(weight_sum)


def blend_kernel(a_ref, b_ref, c_ref, d_ref, out_ref):
    rows, width = a_ref.shape
    heads = width // HEAD_DIM - 1
    cols = heads * HEAD_DIM
    mixed, whole = blend(
        [a_ref[...], b_ref[...], c_ref[...], d_ref[...]], spread_matrix(heads), heads
    )
    out_ref[:, :cols] = mixed.astype(BF16)
    out_ref[:, cols:] = packed_totals(
        [whole[:, head * HEAD_DIM : (head + 1) * HEAD_DIM] for head in range(heads)]
    )


def blend_parts(parts):
    return pl.pallas_call(
        blend_kernel,
        out_shape=shape_of(parts[0].shape),
        in_specs=[VMEM] * 4,
        out_specs=VMEM,
        compiler_params=params(16),
        name="blend",
    )(*parts)


def cross_output_kernel(parts_ref, wo_ref, out_ref):
    heads = parts_ref.shape[2] // HEAD_DIM - 1
    parts = [parts_ref[i] for i in range(parts_ref.shape[0])]
    mixed, _ = blend(parts, spread_matrix(heads), heads)
    out_ref[...] = dot(mixed.astype(BF16), wo_ref[...]).astype(BF16)


def cross_output(parts, wo):
    return pl.pallas_call(
        cross_output_kernel,
        out_shape=shape_of((parts.shape[1], wo.shape[1])),
        in_specs=[VMEM] * 2,
        out_specs=VMEM,
        compiler_params=params(16),
        name="cross_output",
    )(parts, wo)


def self_project_kernel(
    ids_ref, latent_ref, one_ref, two_ref, wq_ref, wk_ref, wv_ref, state_ref, *rest
):
    outs, held = rest[:4], rest[4]
    rows, cols = held.shape[1:]
    state = latent_ref[...].astype(F32) + (one_ref[...].astype(F32) + two_ref[...].astype(F32))
    state_ref[...] = state
    normed = (state * inv_rms(state)).astype(BF16)
    held[0] = (dot(normed, wq_ref[...]) * (HEAD_DIM ** (-0.5) * LOG2E)).astype(BF16)
    held[1] = dot(normed, wk_ref[...]).astype(BF16)
    held[2] = dot(normed, wv_ref[...]).astype(BF16)
    for offset in range(4):
        head = lax.rem(ids_ref[0] + offset, 4)
        span = pl.ds(pl.multiple_of(head * HEAD_DIM, HEAD_DIM), HEAD_DIM)
        for part in range(3):
            outs[offset][:, part * HEAD_DIM : (part + 1) * HEAD_DIM] = held[part, :, span]


def self_project(ids, latent_in, one, two, wq, wk, wv):
    rows, width = latent_in.shape
    return pl.pallas_call(
        self_project_kernel,
        out_shape=[shape_of((rows, width), F32)] + [shape_of((rows, 3 * HEAD_DIM))] * 4,
        in_specs=[SMEM] + [VMEM] * 6,
        out_specs=[VMEM] * 5,
        scratch_shapes=[pltpu.VMEM((3, rows, wq.shape[1]), BF16)],
        compiler_params=params(24),
        name="self_project",
    )(ids, latent_in, one, two, wq, wk, wv)


def self_kernel(ids_ref, a_ref, b_ref, c_ref, d_ref, kv_ref, *outs):
    rows = a_ref.shape[0]
    groups, group_rows, _ = kv_ref.shape
    own_a, own_b, stride_a, stride_b, own_y = (ids_ref[i] for i in (0, 1, 3, 4, 5))
    q = jnp.concatenate([ref[:, :HEAD_DIM] for ref in (a_ref, b_ref, c_ref, d_ref)], axis=0)
    k = jnp.concatenate([kv_ref[i, :, :HEAD_DIM] for i in range(groups)], axis=0)
    v = jnp.concatenate([kv_ref[i, :, HEAD_DIM:] for i in range(groups)], axis=0)
    scores = dot_t(q, k)
    q_row = lax.broadcasted_iota(jnp.int32, scores.shape, 0)
    k_row = lax.broadcasted_iota(jnp.int32, scores.shape, 1)
    shift = rows.bit_length() - 1
    q_a = (own_a - (q_row >> shift)) & 3
    q_place = q_a * stride_a + (q_row & (rows - 1)) + (own_b * stride_b + own_y * rows)
    group = k_row >> (group_rows.bit_length() - 1)
    k_a = (own_a - (k_row >> shift)) & 3
    k_place = k_a * stride_a + (group >> 1) * stride_b + (group & 1) * rows + (k_row & (rows - 1))
    scores = jnp.where(k_place <= q_place, scores, MASKED_SCORE)
    peak = jnp.max(scores, axis=1, keepdims=True)
    probs = jnp.exp2(scores - peak).astype(BF16)
    both = dot(probs, jnp.concatenate([v, jnp.ones(v.shape, BF16)], axis=1))
    result = (both[:, :HEAD_DIM] / both[:, HEAD_DIM:]).astype(BF16)
    for offset in range(4):
        outs[offset][...] = result[offset * rows : (offset + 1) * rows]


def self_attend(ids, parts, kv):
    rows = parts[0].shape[0]
    return pl.pallas_call(
        self_kernel,
        out_shape=[shape_of((rows, HEAD_DIM))] * 4,
        in_specs=[SMEM] + [VMEM] * 5,
        out_specs=[VMEM] * 4,
        compiler_params=params(16),
        name="self_attend",
    )(ids, *parts, kv)


def self_output_kernel(ids_ref, a_ref, b_ref, c_ref, d_ref, wo_ref, out_ref, held):
    for offset, ref in enumerate((a_ref, b_ref, c_ref, d_ref)):
        head = lax.rem(ids_ref[0] + offset, 4)
        held[:, pl.ds(pl.multiple_of(head * HEAD_DIM, HEAD_DIM), HEAD_DIM)] = ref[...]
    out_ref[...] = dot(held[...], wo_ref[...]).astype(BF16)


def self_output(ids, parts, wo):
    rows = parts[0].shape[0]
    return pl.pallas_call(
        self_output_kernel,
        out_shape=shape_of((rows, wo.shape[1])),
        in_specs=[SMEM] + [VMEM] * 5,
        out_specs=VMEM,
        scratch_shapes=[pltpu.VMEM((rows, wo.shape[0]), BF16)],
        compiler_params=params(16),
        name="self_output",
    )(ids, *parts, wo)


def moved(tensor, axis, size, offset):
    return lax.ppermute(tensor, axis, [(i, (i + offset) % size) for i in range(size)])


PLANE = ("x", "z", "core")
WHOLE = ("x", "z", "y_lo", "y_hi", "core")


def turned(tensor, axis, offset):
    pairs = []
    for x in range(4):
        for z in range(4):
            for core in range(2):
                if (axis == "a") == (core == 0):
                    to = ((x + offset) % 4, z)
                else:
                    to = (x, (z + offset) % 4)
                pairs.append(((x * 4 + z) * 2 + core, (to[0] * 4 + to[1]) * 2 + core))
    return lax.ppermute(tensor, PLANE, pairs)


def exchanged(tensor):
    order = np.arange(128).reshape(4, 4, 2, 2, 2)
    groups = []
    for y_hi in range(2):
        for a in range(4):
            groups.append(order[a, :, :, y_hi, 0].reshape(-1).tolist())
            groups.append(order[:, a, :, y_hi, 1].reshape(-1).tolist())
    return lax.all_to_all(tensor, WHOLE, 0, 0, axis_index_groups=groups)


def summed_over_tp(part):
    other = moved(part, "core", 2, 1)
    pair = (part.astype(F32) + other.astype(F32)).astype(BF16)
    return pair, moved(pair, "y_hi", 2, 1)


def on_device(
    context,
    latent_in,
    cutoff,
    wq_cross,
    wk_cross,
    wv_cross,
    wo_cross,
    wq_self,
    wk_self,
    wv_self,
    wo_self,
):
    x, z, y_lo = lax.axis_index("x"), lax.axis_index("z"), lax.axis_index("y_lo")
    first_core = lax.axis_index("core") == 0
    a = jnp.where(first_core, x, z)
    b = jnp.where(first_core, z, x)
    rows = latent_in.shape[0]
    stride_a = jnp.where(first_core, 8 * rows, 2 * rows)
    stride_b = jnp.where(first_core, 2 * rows, 8 * rows)
    first_pos = ((x * 4 + z) * 2 + y_lo) * context.shape[0]
    ids = jnp.stack([a, b, first_pos, stride_a, stride_b, y_lo]).astype(jnp.int32)
    turned_cutoff = cutoff.reshape(4, 4, 2 * rows).transpose(1, 0, 2).reshape(-1)
    cutoff = jnp.where(first_core, cutoff, turned_cutoff)
    cut_wide = jnp.broadcast_to(cutoff[:, None], (cutoff.shape[0], HEAD_DIM))

    own = project_queries(latent_in, wq_cross)
    other = moved(own, "y_lo", 2, 1)
    pair = jnp.where(
        y_lo == 0, jnp.concatenate([own, other]), jnp.concatenate([other, own])
    )
    whole = context.shape[0]
    part = whole // 2
    keys = [first_project(context, wk_cross, pair, part)]
    came = {offset: turned(pair, "b", offset) for offset in (2, 1, 3)}
    ring = [pair] + [came[offset] for offset in (1, 2, 3)]
    pieces = [
        lax.dynamic_index_in_dim(jnp.stack(ring), (b - place) & 3, 0, False) for place in range(4)
    ]
    mine = jnp.concatenate(pieces)
    keys.append(project_context(context, wk_cross, mine, "keys", part, whole - part))
    values = project_context(context, wv_cross, mine, "values", 0, whole)
    blocks = {0: mine}
    for offset in (2, 3, 1):
        blocks[(4 - offset) % 4] = turned(mine, "a", offset)

    parts = []
    for offsets in ((2, 1), (3,), (0,)):
        queries = [blocks[offset] for offset in offsets]
        made = cross_attend(offsets, ids, cutoff, queries, keys, values, cut_wide)
        for offset, part in zip(offsets, made):
            parts.append(turned(part, "a", offset) if offset else part)
    mixed = blend_parts(parts)
    mixed = mixed.reshape(8, rows, mixed.shape[1])
    mixed = exchanged(mixed)
    cross_part = cross_output(mixed, wo_cross)
    one, two = summed_over_tp(cross_part)

    state, *sent = self_project(ids, latent_in, one, two, wq_self, wk_self, wv_self)
    came = {o: turned(sent[o], "a", o) for o in (2, 1, 3)}
    parts = [sent[0]] + [came[o] for o in (1, 2, 3)]
    kv = jnp.concatenate([part[:, HEAD_DIM:] for part in parts])
    kv = exchanged(jnp.broadcast_to(kv[None], (8,) + kv.shape))
    outs = self_attend(ids, parts, kv)
    came = {o: turned(outs[o], "a", -o) for o in (2, 1, 3)}
    outs = [outs[0]] + [came[o] for o in (1, 2, 3)]
    self_part = self_output(ids, outs, wo_self)
    one, two = summed_over_tp(self_part)
    return (state + (one.astype(F32) + two.astype(F32))).astype(BF16)


def solution(mesh):
    fine = Mesh(
        mesh.devices.reshape(4, 4, 2, 2, 2), ("x", "z", "y_lo", "y_hi", "core")
    )
    seq, tp = ("x", "z", "y_lo"), ("y_hi", "core")
    in_specs = (
        P(seq, None),
        P(seq, None),
        P(),
        P(None, tp),
        P(None, tp),
        P(None, tp),
        P(tp, None),
        P(None, tp),
        P(None, tp),
        P(None, tp),
        P(tp, None),
    )
    return jax.shard_map(
        on_device, mesh=fine, in_specs=in_specs, out_specs=P(seq, None), check_vma=False
    )
```

```python
import functools

import jax
import jax.numpy as jnp
import numpy as np
from jax import lax
from jax.experimental import pallas as pl
from jax.experimental.pallas import tpu as pltpu
from jax.sharding import Mesh, PartitionSpec as P

HEAD_DIM = 128
EPSILON = 1e-05
MASKED_SCORE = -1e30
LOG2E = 1.4426950408889634
MIB = 1 << 20
F32 = jnp.float32
BF16 = jnp.bfloat16

VMEM = pl.BlockSpec(memory_space=pltpu.VMEM)
HBM = pl.BlockSpec(memory_space=pltpu.HBM)
SMEM = pl.BlockSpec(memory_space=pltpu.SMEM)


def shape_of(dims, dtype=BF16):
    return jax.ShapeDtypeStruct(dims, dtype)


def params(mib):
    return pltpu.CompilerParams(vmem_limit_bytes=mib * MIB)


def cost(flops, nbytes, trans=0):
    return pl.CostEstimate(flops=flops, bytes_accessed=nbytes, transcendentals=trans)


def dot(a, b):
    return jnp.dot(a, b, preferred_element_type=F32)


def dot_t(a, b):
    return lax.dot_general(a, b, (((1,), (1,)), ((), ())), preferred_element_type=F32)


def inv_rms(tile):
    return lax.rsqrt(jnp.mean(tile * tile, axis=-1, keepdims=True) + EPSILON)


def query_kernel(latent_ref, wq_ref, out_ref, latent, weight, sems):
    pieces = weight.shape[0]
    depth = weight.shape[1]
    first = pltpu.make_async_copy(latent_ref, latent, sems.at[pieces])
    copies = [
        pltpu.make_async_copy(wq_ref.at[pl.ds(i * depth, depth)], weight.at[i], sems.at[i])
        for i in range(pieces)
    ]
    for copy in [first] + copies:
        copy.start()
    first.wait()
    tile = latent[...].astype(F32)
    normed = (tile * inv_rms(tile)).astype(BF16)
    total = jnp.zeros(out_ref.shape, F32)
    for i, copy in enumerate(copies):
        copy.wait()
        total += dot(normed[:, i * depth : (i + 1) * depth], weight[i])
    out_ref[...] = (total * (HEAD_DIM ** (-0.5) * LOG2E)).astype(BF16)


def project_queries(latent_in, wq):
    rows, width = latent_in.shape
    cols = wq.shape[1]
    pieces = 4
    return pl.pallas_call(
        query_kernel,
        out_shape=shape_of((rows, cols)),
        in_specs=[HBM, HBM],
        out_specs=VMEM,
        scratch_shapes=[
            pltpu.VMEM((rows, width), BF16),
            pltpu.VMEM((pieces, width // pieces, cols), BF16),
            pltpu.SemaphoreType.DMA((pieces + 1,)),
        ],
        compiler_params=params(20),
        cost_estimate=cost(2 * rows * width * cols, 2 * width * cols),
        name="queries",
    )(
        pltpu.with_memory_space_constraint(latent_in, pltpu.HBM),
        pltpu.with_memory_space_constraint(wq, pltpu.HBM),
    )


def context_kernel(first, step, context_ref, w_ref, after_ref, out_ref):
    def rows_from(i, _):
        there = pl.ds(pl.multiple_of(first + i * step, 128), step)
        tile = context_ref[there, :]
        product = dot(tile, w_ref[...]) * inv_rms(tile.astype(F32))
        out_ref[pl.ds(pl.multiple_of(i * step, 128), step), :] = product.astype(BF16)
        return 0

    lax.fori_loop(0, out_ref.shape[0] // step, rows_from, 0, unroll=True)


def project_context(context, weight, after, name, first, rows):
    width = context.shape[1]
    cols = weight.shape[1]
    return pl.pallas_call(
        functools.partial(context_kernel, first, 512 if rows % 512 == 0 else rows // 2),
        out_shape=shape_of((rows, cols)),
        in_specs=[VMEM, VMEM, pl.BlockSpec(memory_space=pl.ANY)],
        out_specs=VMEM,
        compiler_params=params(20),
        cost_estimate=cost(2 * rows * width * cols, 2 * (rows * width + width * cols)),
        name=name,
    )(context, weight, after)


def first_kernel(context_ref, w_ref, after_ref, out_ref, held, sems):
    pieces, step = held.shape[:2]
    copies = [
        pltpu.make_async_copy(context_ref.at[pl.ds(i * step, step)], held.at[i], sems.at[i])
        for i in range(pieces)
    ]
    for copy in copies:
        copy.start()
    for i, copy in enumerate(copies):
        copy.wait()
        tile = held[i]
        product = dot(tile, w_ref[...]) * inv_rms(tile.astype(F32))
        out_ref[pl.ds(i * step, step), :] = product.astype(BF16)


def first_project(context, weight, after, rows):
    width = context.shape[1]
    cols = weight.shape[1]
    pieces = 3
    return pl.pallas_call(
        first_kernel,
        out_shape=shape_of((rows, cols)),
        in_specs=[HBM, VMEM, pl.BlockSpec(memory_space=pl.ANY)],
        out_specs=VMEM,
        scratch_shapes=[
            pltpu.VMEM((pieces, rows // pieces, width), BF16),
            pltpu.SemaphoreType.DMA((pieces,)),
        ],
        compiler_params=params(20),
        cost_estimate=cost(2 * rows * width * cols, 2 * (rows * width + width * cols)),
        name="first_keys",
    )(pltpu.with_memory_space_constraint(context, pltpu.HBM), weight, after)


def packed_totals(totals):
    lane = lax.broadcasted_iota(jnp.int32, totals[0].shape, 1)
    held = jnp.zeros(totals[0].shape, F32)
    for head, total in enumerate(totals):
        held = jnp.where(lane == head, total, held)
    high = held.astype(BF16).astype(F32)
    rest = held - high
    mid = rest.astype(BF16).astype(F32)
    low = rest - mid
    return (high + pltpu.roll(mid, 4, 1) + pltpu.roll(low, 8, 1)).astype(BF16)


def spread_matrix(heads):
    dims = (HEAD_DIM, heads * HEAD_DIM)
    row = lax.broadcasted_iota(jnp.int32, dims, 0)
    head = lax.broadcasted_iota(jnp.int32, dims, 1) >> 7
    return jnp.where((row < 12) & ((row & 3) == head), 1.0, 0.0).astype(BF16)


def cross_kernel(offsets, ids_ref, cutoff_ref, cut_ref, k_ref, more_ref, v_ref, *rest):
    blocks = len(offsets)
    q_refs, out_refs, bias = rest[:blocks], rest[blocks : 2 * blocks], rest[2 * blocks]
    rows, cols = q_refs[0].shape
    heads = cols // HEAD_DIM
    places = v_ref.shape[0]
    step = 512
    first_pos = ids_ref[2]
    starts = [((ids_ref[0] + offset) & 3) * rows for offset in offsets]
    lowest = functools.reduce(jnp.minimum, [cutoff_ref[start] for start in starts])
    highest = functools.reduce(jnp.maximum, [cutoff_ref[start + rows - 1] for start in starts])
    lowest, highest = lowest - first_pos, highest - first_pos
    spans = [slice(head * HEAD_DIM, (head + 1) * HEAD_DIM) for head in range(heads)]

    def stacked(pieces):
        return pieces[0] if blocks == 1 else jnp.concatenate(pieces, axis=0)

    def put(span, value):
        for i, out_ref in enumerate(out_refs):
            out_ref[:, span] = value[i * rows : (i + 1) * rows].astype(BF16)

    @pl.when(highest < 0)
    def _():
        put(slice(0, cols), jnp.zeros((blocks * rows, cols), BF16))
        put(
            slice(cols, cols + HEAD_DIM),
            packed_totals([jnp.full((blocks * rows, HEAD_DIM), MASKED_SCORE, F32)] * heads),
        )

    def attend(masked):
        ones = jnp.ones((step, HEAD_DIM), BF16)
        if masked:
            cut = stacked(
                [cut_ref[pl.ds(pl.multiple_of(start, rows), rows), :] for start in starts]
            )
            cut = cut - first_pos
            order = lax.broadcasted_iota(jnp.int32, cut.shape, 1)
            for place in range(0, places, HEAD_DIM):
                bias[:, place : place + HEAD_DIM] = jnp.where(
                    order + place <= cut, 0.0, MASKED_SCORE
                )

        def scores_of(head):
            queries = stacked([q_ref[:, spans[head]] for q_ref in q_refs])
            keys = jnp.concatenate([k_ref[:, spans[head]], more_ref[:, spans[head]]], axis=0)
            scores = dot_t(queries, keys)
            return scores + bias[...] if masked else scores

        totals = []
        scores = scores_of(0)
        for head in range(heads):
            peak = jnp.max(scores, axis=1, keepdims=True)
            later = scores_of(head + 1) if head + 1 < heads else None
            both = jnp.zeros((blocks * rows, 2 * HEAD_DIM), F32)
            for place in range(0, places, step):
                here = slice(place, place + step)
                probs = jnp.exp2(scores[:, here] - peak).astype(BF16)
                both += dot(probs, jnp.concatenate([v_ref[here, spans[head]], ones], axis=1))
            total = both[:, HEAD_DIM:]
            put(spans[head], both[:, :HEAD_DIM] / total)
            whole = jnp.log2(total) + peak
            totals.append(jnp.where(cut >= 0, whole, MASKED_SCORE) if masked else whole)
            scores = later
        put(slice(cols, cols + HEAD_DIM), packed_totals(totals))

    @pl.when(highest >= 0)
    def _():
        attend(True)


def cross_attend(offsets, ids, cutoff, queries, keys, values, cut_wide):
    blocks = len(offsets)
    rows, cols = queries[0].shape
    places = values.shape[0]
    return pl.pallas_call(
        functools.partial(cross_kernel, offsets),
        out_shape=[shape_of((rows, cols + HEAD_DIM))] * blocks,
        in_specs=[SMEM, SMEM] + [VMEM] * (4 + blocks),
        out_specs=[VMEM] * blocks,
        scratch_shapes=[pltpu.VMEM((blocks * rows, places), F32)],
        compiler_params=params(20 if blocks == 1 else 32),
        cost_estimate=cost(
            blocks * 8 * rows * places * cols, 4 * places * cols, blocks * rows * places * 4
        ),
        name="cross",
    )(ids, cutoff, cut_wide, *keys, values, *queries)


def blend(parts, spread, heads):
    cols = heads * HEAD_DIM
    totals = [dot(part[:, cols:], spread) for part in parts]
    peak = functools.reduce(jnp.maximum, totals)
    weights = [jnp.exp2(total - peak) for total in totals]
    weight_sum = functools.reduce(jnp.add, weights)
    mixed = functools.reduce(
        jnp.add, [w * part[:, :cols].astype(F32) for w, part in zip(weights, parts)]
    )
    return mixed / weight_sum, peak + jnp.log2(weight_sum)


def blend_kernel(a_ref, b_ref, c_ref, d_ref, out_ref):
    rows, width = a_ref.shape
    heads = width // HEAD_DIM - 1
    cols = heads * HEAD_DIM
    mixed, whole = blend(
        [a_ref[...], b_ref[...], c_ref[...], d_ref[...]], spread_matrix(heads), heads
    )
    out_ref[:, :cols] = mixed.astype(BF16)
    out_ref[:, cols:] = packed_totals(
        [whole[:, head * HEAD_DIM : (head + 1) * HEAD_DIM] for head in range(heads)]
    )


def blend_parts(parts):
    return pl.pallas_call(
        blend_kernel,
        out_shape=shape_of(parts[0].shape),
        in_specs=[VMEM] * 4,
        out_specs=VMEM,
        compiler_params=params(16),
        name="blend",
    )(*parts)


def cross_output_kernel(parts_ref, wo_ref, out_ref):
    heads = parts_ref.shape[2] // HEAD_DIM - 1
    parts = [parts_ref[i] for i in range(parts_ref.shape[0])]
    mixed, _ = blend(parts, spread_matrix(heads), heads)
    out_ref[...] = dot(mixed.astype(BF16), wo_ref[...]).astype(BF16)


def cross_output(parts, wo):
    return pl.pallas_call(
        cross_output_kernel,
        out_shape=shape_of((parts.shape[1], wo.shape[1])),
        in_specs=[VMEM] * 2,
        out_specs=VMEM,
        compiler_params=params(16),
        name="cross_output",
    )(parts, wo)


def self_project_kernel(
    ids_ref, latent_ref, one_ref, two_ref, wq_ref, wk_ref, wv_ref, state_ref, *rest
):
    outs, held = rest[:4], rest[4]
    rows, cols = held.shape[1:]
    state = latent_ref[...].astype(F32) + (one_ref[...].astype(F32) + two_ref[...].astype(F32))
    state_ref[...] = state
    normed = (state * inv_rms(state)).astype(BF16)
    held[0] = (dot(normed, wq_ref[...]) * (HEAD_DIM ** (-0.5) * LOG2E)).astype(BF16)
    held[1] = dot(normed, wk_ref[...]).astype(BF16)
    held[2] = dot(normed, wv_ref[...]).astype(BF16)
    for offset in range(4):
        head = lax.rem(ids_ref[0] + offset, 4)
        span = pl.ds(pl.multiple_of(head * HEAD_DIM, HEAD_DIM), HEAD_DIM)
        for part in range(3):
            outs[offset][:, part * HEAD_DIM : (part + 1) * HEAD_DIM] = held[part, :, span]


def self_project(ids, latent_in, one, two, wq, wk, wv):
    rows, width = latent_in.shape
    return pl.pallas_call(
        self_project_kernel,
        out_shape=[shape_of((rows, width), F32)] + [shape_of((rows, 3 * HEAD_DIM))] * 4,
        in_specs=[SMEM] + [VMEM] * 6,
        out_specs=[VMEM] * 5,
        scratch_shapes=[pltpu.VMEM((3, rows, wq.shape[1]), BF16)],
        compiler_params=params(24),
        name="self_project",
    )(ids, latent_in, one, two, wq, wk, wv)


def self_kernel(ids_ref, a_ref, b_ref, c_ref, d_ref, kv_ref, *outs):
    rows = a_ref.shape[0]
    groups, group_rows, _ = kv_ref.shape
    own_a, own_b, stride_a, stride_b, own_y = (ids_ref[i] for i in (0, 1, 3, 4, 5))
    q = jnp.concatenate([ref[:, :HEAD_DIM] for ref in (a_ref, b_ref, c_ref, d_ref)], axis=0)
    k = jnp.concatenate([kv_ref[i, :, :HEAD_DIM] for i in range(groups)], axis=0)
    v = jnp.concatenate([kv_ref[i, :, HEAD_DIM:] for i in range(groups)], axis=0)
    scores = dot_t(q, k)
    q_row = lax.broadcasted_iota(jnp.int32, scores.shape, 0)
    k_row = lax.broadcasted_iota(jnp.int32, scores.shape, 1)
    shift = rows.bit_length() - 1
    q_a = (own_a - (q_row >> shift)) & 3
    q_place = q_a * stride_a + (q_row & (rows - 1)) + (own_b * stride_b + own_y * rows)
    group = k_row >> (group_rows.bit_length() - 1)
    k_a = (own_a - (k_row >> shift)) & 3
    k_place = k_a * stride_a + (group >> 1) * stride_b + (group & 1) * rows + (k_row & (rows - 1))
    scores = jnp.where(k_place <= q_place, scores, MASKED_SCORE)
    peak = jnp.max(scores, axis=1, keepdims=True)
    probs = jnp.exp2(scores - peak).astype(BF16)
    both = dot(probs, jnp.concatenate([v, jnp.ones(v.shape, BF16)], axis=1))
    result = (both[:, :HEAD_DIM] / both[:, HEAD_DIM:]).astype(BF16)
    for offset in range(4):
        outs[offset][...] = result[offset * rows : (offset + 1) * rows]


def self_attend(ids, parts, kv):
    rows = parts[0].shape[0]
    return pl.pallas_call(
        self_kernel,
        out_shape=[shape_of((rows, HEAD_DIM))] * 4,
        in_specs=[SMEM] + [VMEM] * 5,
        out_specs=[VMEM] * 4,
        compiler_params=params(16),
        name="self_attend",
    )(ids, *parts, kv)


def self_output_kernel(ids_ref, a_ref, b_ref, c_ref, d_ref, wo_ref, out_ref, held):
    for offset, ref in enumerate((a_ref, b_ref, c_ref, d_ref)):
        head = lax.rem(ids_ref[0] + offset, 4)
        held[:, pl.ds(pl.multiple_of(head * HEAD_DIM, HEAD_DIM), HEAD_DIM)] = ref[...]
    out_ref[...] = dot(held[...], wo_ref[...]).astype(BF16)


def self_output(ids, parts, wo):
    rows = parts[0].shape[0]
    return pl.pallas_call(
        self_output_kernel,
        out_shape=shape_of((rows, wo.shape[1])),
        in_specs=[SMEM] + [VMEM] * 5,
        out_specs=VMEM,
        scratch_shapes=[pltpu.VMEM((rows, wo.shape[0]), BF16)],
        compiler_params=params(16),
        name="self_output",
    )(ids, *parts, wo)


def moved(tensor, axis, size, offset):
    return lax.ppermute(tensor, axis, [(i, (i + offset) % size) for i in range(size)])


PLANE = ("x", "z", "core")
WHOLE = ("x", "z", "y_lo", "y_hi", "core")


def turned(tensor, axis, offset):
    pairs = []
    for x in range(4):
        for z in range(4):
            for core in range(2):
                if (axis == "a") == (core == 0):
                    to = ((x + offset) % 4, z)
                else:
                    to = (x, (z + offset) % 4)
                pairs.append(((x * 4 + z) * 2 + core, (to[0] * 4 + to[1]) * 2 + core))
    return lax.ppermute(tensor, PLANE, pairs)


def exchanged(tensor):
    order = np.arange(128).reshape(4, 4, 2, 2, 2)
    groups = []
    for y_hi in range(2):
        for a in range(4):
            groups.append(order[a, :, :, y_hi, 0].reshape(-1).tolist())
            groups.append(order[:, a, :, y_hi, 1].reshape(-1).tolist())
    return lax.all_to_all(tensor, WHOLE, 0, 0, axis_index_groups=groups)


def summed_over_tp(part):
    other = moved(part, "core", 2, 1)
    pair = (part.astype(F32) + other.astype(F32)).astype(BF16)
    return pair, moved(pair, "y_hi", 2, 1)


def on_device(
    context,
    latent_in,
    cutoff,
    wq_cross,
    wk_cross,
    wv_cross,
    wo_cross,
    wq_self,
    wk_self,
    wv_self,
    wo_self,
):
    x, z, y_lo = lax.axis_index("x"), lax.axis_index("z"), lax.axis_index("y_lo")
    first_core = lax.axis_index("core") == 0
    a = jnp.where(first_core, x, z)
    b = jnp.where(first_core, z, x)
    rows = latent_in.shape[0]
    stride_a = jnp.where(first_core, 8 * rows, 2 * rows)
    stride_b = jnp.where(first_core, 2 * rows, 8 * rows)
    first_pos = ((x * 4 + z) * 2 + y_lo) * context.shape[0]
    ids = jnp.stack([a, b, first_pos, stride_a, stride_b, y_lo]).astype(jnp.int32)
    turned_cutoff = cutoff.reshape(4, 4, 2 * rows).transpose(1, 0, 2).reshape(-1)
    cutoff = jnp.where(first_core, cutoff, turned_cutoff)
    cut_wide = jnp.broadcast_to(cutoff[:, None], (cutoff.shape[0], HEAD_DIM))

    own = project_queries(latent_in, wq_cross)
    other = moved(own, "y_lo", 2, 1)
    pair = jnp.where(
        y_lo == 0, jnp.concatenate([own, other]), jnp.concatenate([other, own])
    )
    whole = context.shape[0]
    part = whole // 8 * 3
    keys = [first_project(context, wk_cross, pair, part)]
    came = {offset: turned(pair, "b", offset) for offset in (2, 1, 3)}
    ring = [pair] + [came[offset] for offset in (1, 2, 3)]
    pieces = [
        lax.dynamic_index_in_dim(jnp.stack(ring), (b - place) & 3, 0, False) for place in range(4)
    ]
    mine = jnp.concatenate(pieces)
    keys.append(project_context(context, wk_cross, mine, "keys", part, whole - part))
    values = project_context(context, wv_cross, mine, "values", 0, whole)
    blocks = {0: mine}
    for offset in (2, 3, 1):
        blocks[(4 - offset) % 4] = turned(mine, "a", offset)

    parts = []
    for offsets in ((2, 1), (3,), (0,)):
        queries = [blocks[offset] for offset in offsets]
        made = cross_attend(offsets, ids, cutoff, queries, keys, values, cut_wide)
        for offset, part in zip(offsets, made):
            parts.append(turned(part, "a", offset) if offset else part)
    mixed = blend_parts(parts)
    mixed = mixed.reshape(8, rows, mixed.shape[1])
    mixed = exchanged(mixed)
    cross_part = cross_output(mixed, wo_cross)
    one, two = summed_over_tp(cross_part)

    state, *sent = self_project(ids, latent_in, one, two, wq_self, wk_self, wv_self)
    came = {o: turned(sent[o], "a", o) for o in (2, 1, 3)}
    parts = [sent[0]] + [came[o] for o in (1, 2, 3)]
    kv = jnp.concatenate([part[:, HEAD_DIM:] for part in parts])
    kv = exchanged(jnp.broadcast_to(kv[None], (8,) + kv.shape))
    outs = self_attend(ids, parts, kv)
    came = {o: turned(outs[o], "a", -o) for o in (2, 1, 3)}
    outs = [outs[0]] + [came[o] for o in (1, 2, 3)]
    self_part = self_output(ids, outs, wo_self)
    one, two = summed_over_tp(self_part)
    return (state + (one.astype(F32) + two.astype(F32))).astype(BF16)


def solution(mesh):
    fine = Mesh(
        mesh.devices.reshape(4, 4, 2, 2, 2), ("x", "z", "y_lo", "y_hi", "core")
    )
    seq, tp = ("x", "z", "y_lo"), ("y_hi", "core")
    in_specs = (
        P(seq, None),
        P(seq, None),
        P(),
        P(None, tp),
        P(None, tp),
        P(None, tp),
        P(tp, None),
        P(None, tp),
        P(None, tp),
        P(None, tp),
        P(tp, None),
    )
    return jax.shard_map(
        on_device, mesh=fine, in_specs=in_specs, out_specs=P(seq, None), check_vma=False
    )
```
